32 devices in a mesh: groups: 2 (over y), row: 4 (over z), col: 2 (over x), mpo: 2 (over core).
Axes of the slice: x: 2, y: 2, z: 4, core: 2. Of those that a mesh axis runs over, the one named last changes fastest.
Arguments:
- start: float32 [6144, 256], P(('groups', 'row'), 'col'), parts along dimension 0, may hold values from -30 to 30
- left_env: bfloat16 [14, 6144, 256], P('mpo', ('groups', 'row')), parts along dimension 1, may hold values from -1.5 to 3
- right_env: bfloat16 [14, 6144, 256], P('mpo', ('groups', 'row'), 'col'), parts along dimension 1, may hold values from -2.5 to 4
- send_list: int32 [8, 4], P(('groups', 'row')), parts along dimension 0, may hold values from -1 to 2, as said below
- term_source: int32 [24, 14], P(('groups', 'row'), 'mpo'), parts along dimension 0, may hold values from 0 to 6, as said below
- sector_len: int32 [24], P(('groups', 'row')), parts along dimension 0, may hold values from 128 to 256
Outputs:
- residual: float32 [6144, 256], P(('groups', 'row'), 'col'), parts along dimension 0
- coefficients: float32 [10], P('groups'), parts along dimension 0
The draws below stay inside these ranges and needn't reach their ends.
There are 2 independent parts, one for each index of `groups`. The reference program is written for one: setup_inputs(seed, part) draws one part's arguments, and reference() takes and returns one part's arrays. A program takes and returns all parts, laid end to end along the dimension named above; each array names one. Nothing has to cross between parts.
Inputs may be any that keep to these rules, and one draw needn't show every extreme that they name: `send_list`: entry [s, d + c] is -1 where s sends nothing in slot c, and always -1 where s = d. `term_source`: an entry of 3 or more names a slot whose send_list entry is not -1.
All inputs are finite; a program needn't handle non-finite values.
Results may differ from the reference program's by a relative error of at most 0.004.
Values may be sent and summed in bfloat16 or wider, within the bound.
A program may use at most 64 MiB of HBM per device.

```python
import jax
import jax.numpy as jnp
from jax import lax

S = 256
K = 14
SEC_DEV = 3
CAP = 1
NSEC = 12
N_ROW = 4


def routing_tables(key):
    key_send = jax.random.fold_in(key, 11)
    key_pick = jax.random.fold_in(key, 12)
    key_own = jax.random.fold_in(key, 13)
    raw = jax.random.randint(key_send, (N_ROW, N_ROW, CAP), 0, 2 * SEC_DEV) - SEC_DEV
    sends = jnp.where(raw >= 0, raw, -1)
    diag = jnp.arange(N_ROW)[:, None, None] == jnp.arange(N_ROW)[None, :, None]
    sends = jnp.where(diag, -1, sends).astype(jnp.int32)
    received = (jnp.transpose(sends, (1, 0, 2)) >= 0).reshape(N_ROW, N_ROW * CAP)
    usable = jnp.concatenate([jnp.ones((N_ROW, SEC_DEV), dtype=bool), received], axis=1)
    usable = jnp.repeat(usable, SEC_DEV, axis=0)[:, None, :]
    pool = SEC_DEV + N_ROW * CAP
    scores = jax.random.randint(key_pick, (NSEC, K, pool), 0, 4096) * pool + jnp.arange(pool)[None, None, :]
    scores = jnp.where(usable, scores, -1)
    picks = jnp.argmax(scores, axis=-1).astype(jnp.int32)
    own = jnp.arange(NSEC, dtype=jnp.int32) % SEC_DEV
    keep_own = jax.random.randint(key_own, (NSEC,), 0, 8) > 0
    first_pick = jnp.where(keep_own, own, picks[:, 0]).astype(jnp.int32)
    picks = jnp.concatenate([first_pick[:, None], picks[:, 1:]], axis=1).astype(jnp.int32)
    return (sends.reshape(N_ROW, N_ROW * CAP), picks)


def draw_send_list(key, part):
    return routing_tables(key)[0]


def draw_term_source(key, part):
    return routing_tables(key)[1]


def rising_rows(base):
    position = (jnp.arange(NSEC * S) // S).astype(jnp.float32) / max(NSEC - 1, 1)
    return (base ** position)[:, None]


def draw_start(key, part):
    key = jax.random.fold_in(key, 21)
    values = jnp.clip(jax.random.normal(key, (NSEC * S, S), jnp.float32), -6.0, 6.0)
    return (values * rising_rows(5.0)).astype(jnp.float32)


def identity_part():
    inside = jnp.arange(NSEC * S) % S
    ondiag = (inside[:, None] == jnp.arange(S)[None, :]).astype(jnp.float32)
    first = (jnp.arange(K) == 0).astype(jnp.float32)[:, None, None]
    return first * ondiag[None, :, :]


def ramp_rows(low):
    inside = (jnp.arange(NSEC * S) % S).astype(jnp.float32) / max(S - 1, 1)
    return (low * 10.0 ** inside)[None, :, None]


def draw_left_env(key, part):
    key = jax.random.fold_in(key, 31)
    noise = jnp.clip(jax.random.normal(key, (K, NSEC * S, S), jnp.float32), -6.0, 6.0)
    values = jnp.clip(noise * S ** (-0.5), -1.5, 1.5) + identity_part()
    return values.astype(jnp.bfloat16)


def draw_right_env(key, part):
    key = jax.random.fold_in(key, 32)
    noise = jnp.clip(jax.random.normal(key, (K, NSEC * S, S), jnp.float32), -6.0, 6.0)
    values = jnp.clip(noise * S ** (-0.5) * ramp_rows(0.2), -2.5, 2.5) + identity_part()
    return values.astype(jnp.bfloat16)


def plant(result, rng, smallest, high):
    longest = result.shape.index(max(result.shape))
    spots = []
    for shift in (0, 1):
        where = [jax.random.randint(jax.random.fold_in(rng, axis), (), 0, length) for axis, length in enumerate(result.shape)]
        where[longest] = (where[longest] + shift) % result.shape[longest]
        spots.append(tuple(where))
    return result.at[spots[0]].set(smallest).at[spots[1]].set(high)


def setup_inputs(seed: int = 0, part: int = 0) -> dict:
    key_list = jax.random.split(jax.random.key(seed), 7)
    part_keys = jax.random.split(jax.random.fold_in(key_list[6], part), 7)
    start = draw_start(jax.random.fold_in(jax.random.fold_in(key_list[6], part), 71), part)
    left_env = draw_left_env(jax.random.fold_in(jax.random.fold_in(key_list[6], part), 71), part)
    right_env = draw_right_env(jax.random.fold_in(jax.random.fold_in(key_list[6], part), 71), part)
    send_list = draw_send_list(jax.random.fold_in(jax.random.fold_in(key_list[6], part), 71), part)
    term_source = draw_term_source(jax.random.fold_in(jax.random.fold_in(key_list[6], part), 71), part)
    sector_len = plant(jax.random.randint(part_keys[5], (NSEC,), S // 2, S + 1), jax.random.fold_in(part_keys[5], 1), S // 2, S).astype(jnp.int32)
    return dict(start=start, left_env=left_env, right_env=right_env, send_list=send_list, term_source=term_source, sector_len=sector_len)


def source_table(send_list, term_source):
    holder = (jnp.arange(NSEC, dtype=jnp.int32) // SEC_DEV)[:, None]
    is_local = term_source < SEC_DEV
    offset = jnp.maximum(term_source - SEC_DEV, 0)
    sender = offset // CAP
    which = send_list[sender, holder * CAP + offset % CAP]
    remote = sender * SEC_DEV + jnp.maximum(which, 0)
    return jnp.where(is_local, holder * SEC_DEV + term_source, remote).astype(jnp.int32)

def reference(start, left_env, right_env, send_list, term_source, sector_len):
    rows = jnp.arange(S, dtype=jnp.int32)[None, :] < sector_len[:, None]
    mask = rows.astype(jnp.float32).reshape(NSEC * S, 1)
    table = source_table(send_list, term_source)
    left = left_env.reshape(K, NSEC, S, S)
    right = right_env.reshape(K, NSEC, S, S)

    def apply(field):
        blocks = field.astype(jnp.bfloat16).reshape(NSEC, S, S)

        def one(sector):
            sources = blocks[table[sector]].astype(jnp.float32)
            lblock = left[:, sector].astype(jnp.float32)
            inner = jnp.einsum('kab,kbc->kac', lblock, sources).astype(jnp.bfloat16)
            inner = lax.optimization_barrier(inner).astype(jnp.float32)
            rblock = right[:, sector].astype(jnp.float32)
            return jnp.einsum('kac,kdc->ad', inner, rblock)
        image = lax.map(one, jnp.arange(NSEC, dtype=jnp.int32))
        return image.reshape(NSEC * S, S) * mask
    first = start * mask
    vector = first / jnp.sqrt(jnp.sum(first * first) + 1e-06)
    previous = jnp.zeros_like(vector)
    beta = jnp.float32(0.0)
    alphas = []
    betas = []
    for step in range(3):
        image = apply(vector)
        alpha = jnp.sum(vector * image)
        resid = image - alpha * vector - beta * previous
        alphas.append(alpha)
        if step < 2:
            beta = jnp.sqrt(jnp.sum(resid * resid) + 1e-06)
            betas.append(beta)
            previous, vector = (vector, resid / beta)
    return (resid, jnp.stack(alphas + betas).astype(jnp.float32))
```

```python
import functools

import jax
import jax.numpy as jnp
from jax import lax
from jax.experimental import pallas as pl
from jax.experimental.pallas import tpu as pltpu
from jax.sharding import PartitionSpec as P

STEPS = 3
LANES = 128
EPS = 1e-06
MESH = pl.DeviceIdType.MESH


def kernel(
    sizes,
    start_ref,
    left_hbm,
    right_hbm,
    send_ref,
    term_ref,
    len_ref,
    resid_ref,
    coef_ref,
    left,
    right,
    right_t,
    field,
    previous,
    image,
    half,
    pool,
    outgoing,
    inner,
    part,
    from_core,
    to_col,
    from_col,
    sums,
    final,
    load_sem,
    core_send,
    core_recv,
    row_send,
    row_recv,
    pass_send,
    pass_recv,
    part_send,
    part_recv,
    col_send,
    col_recv,
    sum_send,
    sum_recv,
    final_send,
    final_recv,
):
    n_row, n_col, n_mpo = sizes
    k_local, _, width = left_hbm.shape
    sec_dev, rows, columns = field.shape
    cap = send_ref.shape[1] // n_row
    stride = right_t.shape[1] // k_local
    total = n_row * n_col * n_mpo
    row = lax.axis_index("row")
    col = lax.axis_index("col")
    mpo = lax.axis_index("mpo")
    other = lax.rem(mpo + 1, 2)
    mine = (row * n_col + col) * n_mpo + mpo
    my_rows = pl.ds(pl.multiple_of(mpo * rows, rows), rows)
    sibling = {"mpo": other}

    def device(index):
        return {
            "row": index // (n_col * n_mpo),
            "col": lax.rem(index // n_mpo, n_col),
            "mpo": lax.rem(index, n_mpo),
        }

    def peer(step):
        return lax.rem(mine + step, total)

    def remote(src, dst, send, recv, target):
        return pltpu.make_async_remote_copy(
            src_ref=src, dst_ref=dst, send_sem=send, recv_sem=recv,
            device_id=target, device_id_type=MESH,
        )

    loads = []
    for p in range(sec_dev):
        at = pl.multiple_of(p * width + mpo * rows, rows)
        loads.append(pltpu.make_async_copy(start_ref.at[pl.ds(at, rows)], field.at[p], load_sem.at[p]))
    load_right = pltpu.make_async_copy(right_hbm, right, load_sem.at[sec_dev])
    load_left = pltpu.make_async_copy(left_hbm, left, load_sem.at[sec_dev + 1])
    for copy in loads:
        copy.start()
    load_right.start()
    load_left.start()

    barrier = pltpu.get_barrier_semaphore()

    def greet(step, carry):
        pl.semaphore_signal(barrier, inc=1, device_id=device(peer(step)), device_id_type=MESH)
        return carry

    lax.fori_loop(1, total, greet, 0)

    live = []
    for p in range(sec_dev):
        position = lax.broadcasted_iota(jnp.int32, (rows, columns), 0) + mpo * rows
        live.append((position < len_ref[p]).astype(jnp.float32))
    for copy in loads:
        copy.wait()
    for p in range(sec_dev):
        field[p] = field[p] * live[p]
    previous[...] = jnp.zeros_like(previous)
    for j in range(STEPS):
        for c in range(cap):
            pool[j, sec_dev + row * cap + c] = jnp.zeros((width, columns), jnp.bfloat16)
    if stride != columns:
        inner[...] = jnp.zeros_like(inner)
        right_t[...] = jnp.zeros_like(right_t)
    pl.semaphore_wait(barrier, total - 1)

    def exchange(j):
        half[...] = field[...].astype(jnp.bfloat16)
        copies = []
        for step in range(1, n_row):
            target = lax.rem(row + step, n_row)
            for c in range(cap):
                slot = (step - 1) * cap + c
                pick = jnp.maximum(send_ref[0, target * cap + c], 0)
                outgoing[slot] = half[pick]
                place = sec_dev + row * cap + c
                copy = remote(
                    outgoing.at[slot], pool.at[j, place, my_rows],
                    row_send.at[slot], row_recv.at[j, row * cap + c], {"row": target},
                )
                copy.start()
                copies.append(copy)
        pool[j, pl.ds(0, sec_dev), my_rows] = half[...]
        own = remote(
            half, pool.at[j, pl.ds(0, sec_dev), my_rows], core_send, core_recv.at[j], sibling
        )
        own.start()
        return copies + [own]

    def relay(j):
        copies = []
        for step in range(1, n_row):
            source = lax.rem(row + step, n_row)
            for c in range(cap):
                slot = (step - 1) * cap + c
                place = sec_dev + source * cap + c
                block = pool.at[j, place, my_rows]
                remote(
                    outgoing.at[slot], block, row_send.at[slot],
                    row_recv.at[j, source * cap + c], {"row": source},
                ).wait_recv()
                copy = remote(
                    block, block, pass_send.at[slot], pass_recv.at[j, source * cap + c], sibling
                )
                copy.start()
                copies.append(copy)
        their_rows = pl.ds(pl.multiple_of(other * rows, rows), rows)
        remote(
            half, pool.at[j, pl.ds(0, sec_dev), their_rows], core_send, core_recv.at[j], sibling
        ).wait_recv()
        for step in range(1, n_row):
            source = lax.rem(row + step, n_row)
            for c in range(cap):
                slot = (step - 1) * cap + c
                block = pool.at[j, sec_dev + source * cap + c, their_rows]
                remote(
                    block, block, pass_send.at[slot], pass_recv.at[j, source * cap + c], sibling
                ).wait_recv()
        return copies

    def product(j, p):
        for k in range(k_local):
            block = pool[j, term_ref[p, k]]
            value = jnp.dot(
                left[k, p * width:(p + 1) * width, :], block, preferred_element_type=jnp.float32
            )
            inner[p, :, k * stride:k * stride + columns] = value.astype(jnp.bfloat16)
        value = jnp.dot(inner[p], right_t[p], preferred_element_type=jnp.float32)
        for m in range(n_mpo):
            for c in range(n_col):
                part[p, m, c] = value[m * rows:(m + 1) * rows, c * columns:(c + 1) * columns]
        copy = remote(
            part.at[p, other], from_core.at[j, p], part_send.at[p], part_recv.at[j, p], sibling
        )
        copy.start()
        return [copy]

    def add_core(j, p):
        remote(
            part.at[p, other], from_core.at[j, p], part_send.at[p], part_recv.at[j, p], sibling
        ).wait_recv()
        copies = []
        for step in range(1, n_col):
            target = lax.rem(col + step, n_col)
            value = part[p, mpo, target] + from_core[j, p, target]
            to_col[p, step - 1] = value.astype(to_col.dtype)
            copy = remote(
                to_col.at[p, step - 1], from_col.at[j, p, col],
                col_send.at[p, step - 1], col_recv.at[j, p, col], {"col": target},
            )
            copy.start()
            copies.append(copy)
        image[p] = part[p, mpo, col] + from_core[j, p, col]
        return copies

    def add_col(j, p):
        value = image[p]
        for step in range(1, n_col):
            source = lax.rem(col + step, n_col)
            remote(
                to_col.at[p, step - 1], from_col.at[j, p, source],
                col_send.at[p, step - 1], col_recv.at[j, p, source], {"col": source},
            ).wait_recv()
            value = value + from_col[j, p, source].astype(jnp.float32)
        value = value * live[p]
        image[p] = value
        return value

    def fold(value):
        return jnp.sum(value.reshape(rows // 8, 8, columns), axis=0)

    def body(j, carry):
        copies = exchange(j)

        @pl.when(j == 0)
        def _():
            load_right.wait()
            for p in range(sec_dev):
                for k in range(k_local):
                    block = right[k, p * width:(p + 1) * width, :]
                    right_t[p, k * stride:k * stride + columns, :] = block.T
            load_left.wait()

        copies += relay(j)
        copies += product(j, 0)
        for p in range(1, sec_dev):
            copies += product(j, p)
            copies += add_core(j, p - 1)
        copies += add_core(j, sec_dev - 1)
        overlap = jnp.zeros((8, columns), jnp.float32)
        norm = jnp.zeros((8, columns), jnp.float32)
        for p in range(sec_dev):
            u = field[p]
            norm = norm + fold(u * u)
            overlap = overlap + fold(u * add_col(j, p))
        sums[j, mine, 0] = overlap
        sums[j, mine, 1] = norm

        def share(step, carry):
            block = sums.at[j, mine]
            remote(
                block, block, sum_send.at[step], sum_recv.at[j, mine], device(peer(step))
            ).start()
            return carry

        lax.fori_loop(1, total, share, 0)

        def collect(step, carry):
            source = peer(step)
            block = sums.at[j, source]
            remote(
                block, block, sum_send.at[step], sum_recv.at[j, source], device(source)
            ).wait_recv()
            return carry

        lax.fori_loop(1, total, collect, 0)
        added = jnp.sum(sums[j], axis=0)
        overlap = jnp.sum(added[0], keepdims=True)
        norm = jnp.sum(added[1], keepdims=True)
        beta = jnp.sqrt(norm + EPS)
        scale = 1.0 / beta
        alpha = overlap * scale * scale
        for p in range(sec_dev):
            v = field[p] * scale
            field[p] = image[p] * scale - alpha * v - beta * previous[p]
            previous[p] = v
        coef_ref[pl.ds(j, 1)] = jnp.broadcast_to(alpha, (1, LANES))
        coef_ref[pl.ds(STEPS - 1 + j, 1)] = jnp.where(
            j > 0, jnp.broadcast_to(beta, (1, LANES)), jnp.broadcast_to(alpha, (1, LANES))
        )

        for copy in copies:
            copy.wait_send()

        def sent(step, carry):
            block = sums.at[j, mine]
            remote(
                block, block, sum_send.at[step], sum_recv.at[j, mine], device(peer(step))
            ).wait_send()
            return carry

        lax.fori_loop(1, total, sent, 0)
        return carry

    lax.fori_loop(0, STEPS, body, 0)

    copy = remote(field, final, final_send, final_recv, sibling)
    copy.start()
    for p in range(sec_dev):
        at = pl.multiple_of(p * width + mpo * rows, rows)
        resid_ref[pl.ds(at, rows)] = field[p]
    copy.wait_recv()
    for p in range(sec_dev):
        at = pl.multiple_of(p * width + other * rows, rows)
        resid_ref[pl.ds(at, rows)] = final[p]
    copy.wait_send()


def on_device(sizes, start, left_env, right_env, send_list, term_source, sector_len):
    n_row, n_col, n_mpo = sizes
    sec_dev = sector_len.shape[0]
    k_local, height, width = left_env.shape
    columns = start.shape[1]
    rows = width // n_mpo
    stride = max(columns, LANES)
    total = n_row * n_col * n_mpo
    slots = send_list.shape[1]
    cap = slots // n_row
    away = max((n_row - 1) * cap, 1)
    bf, f32 = jnp.bfloat16, jnp.float32
    dma = pltpu.SemaphoreType.DMA
    hbm = pl.BlockSpec(memory_space=pl.ANY)
    smem = pl.BlockSpec(memory_space=pltpu.SMEM)
    vmem = pl.BlockSpec(memory_space=pltpu.VMEM)
    send = jnp.bfloat16
    resid, coef = pl.pallas_call(
        functools.partial(kernel, sizes),
        out_shape=(
            jax.ShapeDtypeStruct((height, columns), f32),
            jax.ShapeDtypeStruct((8, LANES), f32),
        ),
        in_specs=[hbm, hbm, hbm, smem, smem, smem],
        out_specs=(vmem, vmem),
        scratch_shapes=[
            pltpu.VMEM((k_local, height, width), bf),
            pltpu.VMEM((k_local, height, columns), bf),
            pltpu.VMEM((sec_dev, k_local * stride, width), bf),
            pltpu.VMEM((sec_dev, rows, columns), f32),
            pltpu.VMEM((sec_dev, rows, columns), f32),
            pltpu.VMEM((sec_dev, rows, columns), f32),
            pltpu.VMEM((sec_dev, rows, columns), bf),
            pltpu.VMEM((STEPS, sec_dev + slots, width, columns), bf),
            pltpu.VMEM((away, rows, columns), bf),
            pltpu.VMEM((sec_dev, width, k_local * stride), bf),
            pltpu.VMEM((sec_dev, n_mpo, n_col, rows, columns), f32),
            pltpu.VMEM((STEPS, sec_dev, n_col, rows, columns), f32),
            pltpu.VMEM((sec_dev, n_col, rows, columns), send),
            pltpu.VMEM((STEPS, sec_dev, n_col, rows, columns), send),
            pltpu.VMEM((STEPS, total, 2, 8, columns), f32),
            pltpu.VMEM((sec_dev, rows, columns), f32),
            dma((sec_dev + 2,)),
            dma,
            dma((STEPS,)),
            dma((away,)),
            dma((STEPS, slots)),
            dma((away,)),
            dma((STEPS, slots)),
            dma((sec_dev,)),
            dma((STEPS, sec_dev)),
            dma((sec_dev, n_col)),
            dma((STEPS, sec_dev, n_col)),
            dma((total,)),
            dma((STEPS, total)),
            dma,
            dma,
        ],
        compiler_params=pltpu.CompilerParams(
            collective_id=0, has_side_effects=True, vmem_limit_bytes=44 * 1024 * 1024
        ),
    )(start, left_env, right_env, send_list, term_source, sector_len)
    return resid, coef[:2 * STEPS - 1, 0]


def solution(mesh):
    placed = (
        P(("groups", "row"), "col"),
        P("mpo", ("groups", "row"), None),
        P("mpo", ("groups", "row"), "col"),
        P(("groups", "row"), None),
        P(("groups", "row"), "mpo"),
        P(("groups", "row")),
    )
    sizes = (mesh.shape["row"], mesh.shape["col"], mesh.shape["mpo"])
    return jax.shard_map(
        functools.partial(on_device, sizes),
        mesh=mesh,
        in_specs=placed,
        out_specs=(P(("groups", "row"), "col"), P("groups")),
        check_vma=False,
    )
```

```python
import functools

import jax
import jax.numpy as jnp
from jax import lax
from jax.experimental import pallas as pl
from jax.experimental.pallas import tpu as pltpu
from jax.sharding import PartitionSpec as P

STEPS = 3
LANES = 128
EPS = 1e-06
MESH = pl.DeviceIdType.MESH


def kernel(
    sizes,
    start_ref,
    left_hbm,
    right_hbm,
    send_ref,
    term_ref,
    len_ref,
    resid_ref,
    coef_ref,
    left,
    right,
    right_t,
    field,
    previous,
    image,
    half,
    pool,
    outgoing,
    inner,
    part,
    from_core,
    to_col,
    from_col,
    team,
    line,
    final,
    load_sem,
    core_send,
    core_recv,
    row_send,
    row_recv,
    pass_send,
    pass_recv,
    part_send,
    part_recv,
    col_send,
    col_recv,
    team_send,
    team_recv,
    line_send,
    line_recv,
    final_send,
    final_recv,
):
    n_row, n_col, n_mpo = sizes
    k_local, _, width = left_hbm.shape
    sec_dev, rows, columns = field.shape
    cap = send_ref.shape[1] // n_row
    stride = right_t.shape[1] // k_local
    members = n_col * n_mpo
    row = lax.axis_index("row")
    col = lax.axis_index("col")
    mpo = lax.axis_index("mpo")
    other = lax.rem(mpo + 1, 2)
    mine = col * n_mpo + mpo
    my_rows = pl.ds(pl.multiple_of(mpo * rows, rows), rows)
    sibling = {"mpo": other}

    team_peers = []
    for step in range(1, members):
        index = lax.rem(mine + step, members)
        team_peers.append((index, {"col": index // n_mpo, "mpo": lax.rem(index, n_mpo)}))
    line_peers = []
    for step in range(1, n_row):
        index = lax.rem(row + step, n_row)
        line_peers.append((index, {"row": index}))

    def remote(src, dst, send, recv, target):
        return pltpu.make_async_remote_copy(
            src_ref=src, dst_ref=dst, send_sem=send, recv_sem=recv,
            device_id=target, device_id_type=MESH,
        )

    loads = []
    for p in range(sec_dev):
        at = pl.multiple_of(p * width + mpo * rows, rows)
        loads.append(pltpu.make_async_copy(start_ref.at[pl.ds(at, rows)], field.at[p], load_sem.at[p]))
    load_right = pltpu.make_async_copy(right_hbm, right, load_sem.at[sec_dev])
    load_left = pltpu.make_async_copy(left_hbm, left, load_sem.at[sec_dev + 1])
    for copy in loads:
        copy.start()
    load_right.start()
    load_left.start()

    barrier = pltpu.get_barrier_semaphore()

    for _, target in team_peers + line_peers:
        pl.semaphore_signal(barrier, inc=1, device_id=target, device_id_type=MESH)

    live = []
    for p in range(sec_dev):
        position = lax.broadcasted_iota(jnp.int32, (rows, columns), 0) + mpo * rows
        live.append((position < len_ref[p]).astype(jnp.float32))
    for copy in loads:
        copy.wait()
    for p in range(sec_dev):
        field[p] = field[p] * live[p]
    previous[...] = jnp.zeros_like(previous)
    for j in range(STEPS):
        for c in range(cap):
            pool[j, sec_dev + row * cap + c] = jnp.zeros((width, columns), jnp.bfloat16)
    if stride != columns:
        inner[...] = jnp.zeros_like(inner)
        right_t[...] = jnp.zeros_like(right_t)
    pl.semaphore_wait(barrier, len(team_peers) + len(line_peers))

    def exchange(j):
        half[...] = field[...].astype(jnp.bfloat16)
        copies = []
        for step in range(1, n_row):
            target = lax.rem(row + step, n_row)
            for c in range(cap):
                slot = (step - 1) * cap + c
                pick = jnp.maximum(send_ref[0, target * cap + c], 0)
                outgoing[slot] = half[pick]
                place = sec_dev + row * cap + c
                copy = remote(
                    outgoing.at[slot], pool.at[j, place, my_rows],
                    row_send.at[slot], row_recv.at[j, row * cap + c], {"row": target},
                )
                copy.start()
                copies.append(copy)
        pool[j, pl.ds(0, sec_dev), my_rows] = half[...]
        own = remote(
            half, pool.at[j, pl.ds(0, sec_dev), my_rows], core_send, core_recv.at[j], sibling
        )
        own.start()
        return copies + [own]

    def relay(j):
        copies = []
        for step in range(1, n_row):
            source = lax.rem(row + step, n_row)
            for c in range(cap):
                slot = (step - 1) * cap + c
                place = sec_dev + source * cap + c
                block = pool.at[j, place, my_rows]
                remote(
                    outgoing.at[slot], block, row_send.at[slot],
                    row_recv.at[j, source * cap + c], {"row": source},
                ).wait_recv()
                copy = remote(
                    block, block, pass_send.at[slot], pass_recv.at[j, source * cap + c], sibling
                )
                copy.start()
                copies.append(copy)
        their_rows = pl.ds(pl.multiple_of(other * rows, rows), rows)
        remote(
            half, pool.at[j, pl.ds(0, sec_dev), their_rows], core_send, core_recv.at[j], sibling
        ).wait_recv()
        for step in range(1, n_row):
            source = lax.rem(row + step, n_row)
            for c in range(cap):
                slot = (step - 1) * cap + c
                block = pool.at[j, sec_dev + source * cap + c, their_rows]
                remote(
                    block, block, pass_send.at[slot], pass_recv.at[j, source * cap + c], sibling
                ).wait_recv()
        return copies

    def product(j, p):
        for k in range(k_local):
            block = pool[j, term_ref[p, k]]
            value = jnp.dot(
                left[k, p * width:(p + 1) * width, :], block, preferred_element_type=jnp.float32
            )
            inner[p, :, k * stride:k * stride + columns] = value.astype(jnp.bfloat16)
        value = jnp.dot(inner[p], right_t[p], preferred_element_type=jnp.float32)
        for m in range(n_mpo):
            for c in range(n_col):
                part[p, m, c] = value[m * rows:(m + 1) * rows, c * columns:(c + 1) * columns]
        copy = remote(
            part.at[p, other], from_core.at[j, p], part_send.at[p], part_recv.at[j, p], sibling
        )
        copy.start()
        return [copy]

    def add_core(j, p):
        remote(
            part.at[p, other], from_core.at[j, p], part_send.at[p], part_recv.at[j, p], sibling
        ).wait_recv()
        copies = []
        for step in range(1, n_col):
            target = lax.rem(col + step, n_col)
            value = part[p, mpo, target] + from_core[j, p, target]
            to_col[p, step - 1] = value.astype(to_col.dtype)
            copy = remote(
                to_col.at[p, step - 1], from_col.at[j, p, col],
                col_send.at[p, step - 1], col_recv.at[j, p, col], {"col": target},
            )
            copy.start()
            copies.append(copy)
        image[p] = part[p, mpo, col] + from_core[j, p, col]
        return copies

    def add_col(j, p):
        value = image[p]
        for step in range(1, n_col):
            source = lax.rem(col + step, n_col)
            remote(
                to_col.at[p, step - 1], from_col.at[j, p, source],
                col_send.at[p, step - 1], col_recv.at[j, p, source], {"col": source},
            ).wait_recv()
            value = value + from_col[j, p, source].astype(jnp.float32)
        value = value * live[p]
        image[p] = value
        return value

    def fold(value):
        return jnp.sum(value.reshape(rows // 8, 8, columns), axis=0)

    def gather(slots, own, peers, send, recv):
        block = slots.at[own]
        copies = []
        for step, (_, target) in enumerate(peers):
            copy = remote(block, block, send.at[step], recv.at[own], target)
            copy.start()
            copies.append(copy)
        for step, (index, target) in enumerate(peers):
            theirs = slots.at[index]
            remote(theirs, theirs, send.at[step], recv.at[index], target).wait_recv()
        return copies

    def body(j, carry):
        copies = exchange(j)
        norm = jnp.zeros((8, columns), jnp.float32)
        for p in range(sec_dev):
            norm = norm + fold(field[p] * field[p])

        @pl.when(j == 0)
        def _():
            load_right.wait()
            for p in range(sec_dev):
                for k in range(k_local):
                    block = right[k, p * width:(p + 1) * width, :]
                    right_t[p, k * stride:k * stride + columns, :] = block.T
            load_left.wait()

        copies += relay(j)
        copies += product(j, 0)
        for p in range(1, sec_dev):
            copies += product(j, p)
            copies += add_core(j, p - 1)
        copies += add_core(j, sec_dev - 1)
        overlap = jnp.zeros((8, columns), jnp.float32)
        for p in range(sec_dev):
            overlap = overlap + fold(field[p] * add_col(j, p))
        team[j, mine] = jnp.concatenate(
            [jnp.sum(overlap, axis=0, keepdims=True), jnp.sum(norm, axis=0, keepdims=True)], axis=0
        )
        copies += gather(team.at[j], mine, team_peers, team_send, team_recv.at[j])
        line[j, row] = jnp.sum(team[j], axis=0)
        copies += gather(line.at[j], row, line_peers, line_send, line_recv.at[j])
        added = jnp.sum(line[j], axis=0)
        overlap = jnp.sum(added[0:1], keepdims=True)
        norm = jnp.sum(added[1:2], keepdims=True)
        beta = jnp.sqrt(norm + EPS)
        scale = 1.0 / beta
        alpha = overlap * scale * scale
        for p in range(sec_dev):
            v = field[p] * scale
            field[p] = image[p] * scale - alpha * v - beta * previous[p]
            previous[p] = v
        coef_ref[pl.ds(j, 1)] = jnp.broadcast_to(alpha, (1, LANES))
        coef_ref[pl.ds(STEPS - 1 + j, 1)] = jnp.where(
            j > 0, jnp.broadcast_to(beta, (1, LANES)), jnp.broadcast_to(alpha, (1, LANES))
        )

        for copy in copies:
            copy.wait_send()

        return carry

    lax.fori_loop(0, STEPS, body, 0)

    copy = remote(field, final, final_send, final_recv, sibling)
    copy.start()
    for p in range(sec_dev):
        at = pl.multiple_of(p * width + mpo * rows, rows)
        resid_ref[pl.ds(at, rows)] = field[p]
    copy.wait_recv()
    for p in range(sec_dev):
        at = pl.multiple_of(p * width + other * rows, rows)
        resid_ref[pl.ds(at, rows)] = final[p]
    copy.wait_send()


def on_device(sizes, start, left_env, right_env, send_list, term_source, sector_len):
    n_row, n_col, n_mpo = sizes
    sec_dev = sector_len.shape[0]
    k_local, height, width = left_env.shape
    columns = start.shape[1]
    rows = width // n_mpo
    stride = max(columns, LANES)
    members = n_col * n_mpo
    slots = send_list.shape[1]
    cap = slots // n_row
    away = max((n_row - 1) * cap, 1)
    bf, f32 = jnp.bfloat16, jnp.float32
    dma = pltpu.SemaphoreType.DMA
    hbm = pl.BlockSpec(memory_space=pl.ANY)
    smem = pl.BlockSpec(memory_space=pltpu.SMEM)
    vmem = pl.BlockSpec(memory_space=pltpu.VMEM)
    send = jnp.bfloat16
    resid, coef = pl.pallas_call(
        functools.partial(kernel, sizes),
        out_shape=(
            jax.ShapeDtypeStruct((height, columns), f32),
            jax.ShapeDtypeStruct((8, LANES), f32),
        ),
        in_specs=[hbm, hbm, hbm, smem, smem, smem],
        out_specs=(vmem, vmem),
        scratch_shapes=[
            pltpu.VMEM((k_local, height, width), bf),
            pltpu.VMEM((k_local, height, columns), bf),
            pltpu.VMEM((sec_dev, k_local * stride, width), bf),
            pltpu.VMEM((sec_dev, rows, columns), f32),
            pltpu.VMEM((sec_dev, rows, columns), f32),
            pltpu.VMEM((sec_dev, rows, columns), f32),
            pltpu.VMEM((sec_dev, rows, columns), bf),
            pltpu.VMEM((STEPS, sec_dev + slots, width, columns), bf),
            pltpu.VMEM((away, rows, columns), bf),
            pltpu.VMEM((sec_dev, width, k_local * stride), bf),
            pltpu.VMEM((sec_dev, n_mpo, n_col, rows, columns), f32),
            pltpu.VMEM((STEPS, sec_dev, n_col, rows, columns), f32),
            pltpu.VMEM((sec_dev, n_col, rows, columns), send),
            pltpu.VMEM((STEPS, sec_dev, n_col, rows, columns), send),
            pltpu.VMEM((STEPS, members, 2, columns), f32),
            pltpu.VMEM((STEPS, n_row, 2, columns), f32),
            pltpu.VMEM((sec_dev, rows, columns), f32),
            dma((sec_dev + 2,)),
            dma,
            dma((STEPS,)),
            dma((away,)),
            dma((STEPS, slots)),
            dma((away,)),
            dma((STEPS, slots)),
            dma((sec_dev,)),
            dma((STEPS, sec_dev)),
            dma((sec_dev, n_col)),
            dma((STEPS, sec_dev, n_col)),
            dma((members,)),
            dma((STEPS, members)),
            dma((n_row,)),
            dma((STEPS, n_row)),
            dma,
            dma,
        ],
        compiler_params=pltpu.CompilerParams(
            collective_id=0, has_side_effects=True, vmem_limit_bytes=56 * 1024 * 1024
        ),
    )(start, left_env, right_env, send_list, term_source, sector_len)
    return resid, coef[:2 * STEPS - 1, 0]


def solution(mesh):
    placed = (
        P(("groups", "row"), "col"),
        P("mpo", ("groups", "row"), None),
        P("mpo", ("groups", "row"), "col"),
        P(("groups", "row"), None),
        P(("groups", "row"), "mpo"),
        P(("groups", "row")),
    )
    sizes = (mesh.shape["row"], mesh.shape["col"], mesh.shape["mpo"])
    return jax.shard_map(
        functools.partial(on_device, sizes),
        mesh=mesh,
        in_specs=placed,
        out_specs=(P(("groups", "row"), "col"), P("groups")),
        check_vma=False,
    )
```

```python
import functools

import jax
import jax.numpy as jnp
from jax import lax
from jax.experimental import pallas as pl
from jax.experimental.pallas import tpu as pltpu
from jax.sharding import PartitionSpec as P

STEPS = 3
LANES = 128
EPS = 1e-06
FLAT = 16
MESH = pl.DeviceIdType.MESH


def kernel(
    sizes,
    start_ref,
    left_hbm,
    right_hbm,
    send_ref,
    term_ref,
    len_ref,
    resid_ref,
    coef_ref,
    left,
    right,
    right_t,
    field,
    previous,
    image,
    half,
    pool,
    outgoing,
    inner,
    part,
    from_core,
    to_col,
    from_col,
    team,
    line,
    final,
    load_sem,
    core_send,
    core_recv,
    row_send,
    row_recv,
    pass_send,
    pass_recv,
    part_send,
    part_recv,
    col_send,
    col_recv,
    team_send,
    team_recv,
    line_send,
    line_recv,
    final_send,
    final_recv,
):
    n_row, n_col, n_mpo = sizes
    k_local, _, width = left_hbm.shape
    sec_dev, rows, columns = field.shape
    cap = send_ref.shape[1] // n_row
    stride = right_t.shape[1] // k_local
    members = n_col * n_mpo
    row = lax.axis_index("row")
    col = lax.axis_index("col")
    mpo = lax.axis_index("mpo")
    other = lax.rem(mpo + 1, 2)
    mine = col * n_mpo + mpo
    my_rows = pl.ds(pl.multiple_of(mpo * rows, rows), rows)
    sibling = {"mpo": other}

    flat = team.shape[1] == n_row * members
    team_peers = []
    for step in range(1, team.shape[1]):
        if flat:
            index = lax.rem(row * members + mine + step, n_row * members)
            target = {
                "row": index // members,
                "col": lax.rem(index // n_mpo, n_col),
                "mpo": lax.rem(index, n_mpo),
            }
        else:
            index = lax.rem(mine + step, members)
            target = {"col": index // n_mpo, "mpo": lax.rem(index, n_mpo)}
        team_peers.append((index, target))
    line_peers = []
    for step in range(1, n_row):
        index = lax.rem(row + step, n_row)
        line_peers.append((index, {"row": index}))
    if flat:
        mine = row * members + mine
    greeted = team_peers if flat else team_peers + line_peers

    def remote(src, dst, send, recv, target):
        return pltpu.make_async_remote_copy(
            src_ref=src, dst_ref=dst, send_sem=send, recv_sem=recv,
            device_id=target, device_id_type=MESH,
        )

    loads = []
    for p in range(sec_dev):
        at = pl.multiple_of(p * width + mpo * rows, rows)
        loads.append(pltpu.make_async_copy(start_ref.at[pl.ds(at, rows)], field.at[p], load_sem.at[p]))
    load_right = pltpu.make_async_copy(right_hbm, right, load_sem.at[sec_dev])
    load_left = pltpu.make_async_copy(left_hbm, left, load_sem.at[sec_dev + 1])
    for copy in loads:
        copy.start()
    load_right.start()
    load_left.start()

    barrier = pltpu.get_barrier_semaphore()

    for _, target in greeted:
        pl.semaphore_signal(barrier, inc=1, device_id=target, device_id_type=MESH)

    live = []
    for p in range(sec_dev):
        position = lax.broadcasted_iota(jnp.int32, (rows, columns), 0) + mpo * rows
        live.append((position < len_ref[p]).astype(jnp.float32))
    for copy in loads:
        copy.wait()
    for p in range(sec_dev):
        field[p] = field[p] * live[p]
    previous[...] = jnp.zeros_like(previous)
    for j in range(STEPS):
        for c in range(cap):
            pool[j, sec_dev + row * cap + c] = jnp.zeros((width, columns), jnp.bfloat16)
    if stride != columns:
        inner[...] = jnp.zeros_like(inner)
        right_t[...] = jnp.zeros_like(right_t)
    pl.semaphore_wait(barrier, len(greeted))

    def exchange(j):
        half[j] = field[...].astype(jnp.bfloat16)
        for step in range(1, n_row):
            target = lax.rem(row + step, n_row)
            for c in range(cap):
                slot = (step - 1) * cap + c
                pick = jnp.maximum(send_ref[0, target * cap + c], 0)
                outgoing[j, slot] = half[j, pick]
                place = sec_dev + row * cap + c
                copy = remote(
                    outgoing.at[j, slot], pool.at[j, place, my_rows],
                    row_send.at[j, slot], row_recv.at[j, row * cap + c], {"row": target},
                )
                copy.start()
        pool[j, pl.ds(0, sec_dev), my_rows] = half[j]
        own = remote(
            half.at[j], pool.at[j, pl.ds(0, sec_dev), my_rows], core_send.at[j], core_recv.at[j], sibling
        )
        own.start()

    def relay(j):
        for step in range(1, n_row):
            source = lax.rem(row + step, n_row)
            for c in range(cap):
                slot = (step - 1) * cap + c
                place = sec_dev + source * cap + c
                block = pool.at[j, place, my_rows]
                remote(
                    outgoing.at[j, slot], block, row_send.at[j, slot],
                    row_recv.at[j, source * cap + c], {"row": source},
                ).wait_recv()
                copy = remote(
                    block, block, pass_send.at[j, slot], pass_recv.at[j, source * cap + c], sibling
                )
                copy.start()
        their_rows = pl.ds(pl.multiple_of(other * rows, rows), rows)
        remote(
            half.at[j], pool.at[j, pl.ds(0, sec_dev), their_rows], core_send.at[j], core_recv.at[j], sibling
        ).wait_recv()
        for step in range(1, n_row):
            source = lax.rem(row + step, n_row)
            for c in range(cap):
                slot = (step - 1) * cap + c
                block = pool.at[j, sec_dev + source * cap + c, their_rows]
                remote(
                    block, block, pass_send.at[j, slot], pass_recv.at[j, source * cap + c], sibling
                ).wait_recv()

    def product(j, p):
        for k in range(k_local):
            block = pool[j, term_ref[p, k]]
            value = jnp.dot(
                left[k, p * width:(p + 1) * width, :], block, preferred_element_type=jnp.float32
            )
            inner[p, :, k * stride:k * stride + columns] = value.astype(jnp.bfloat16)
        value = jnp.dot(inner[p], right_t[p], preferred_element_type=jnp.float32)
        for m in range(n_mpo):
            for c in range(n_col):
                part[j, p, m, c] = value[m * rows:(m + 1) * rows, c * columns:(c + 1) * columns]
        copy = remote(
            part.at[j, p, other], from_core.at[j, p], part_send.at[j, p], part_recv.at[j, p], sibling
        )
        copy.start()

    def add_core(j, p):
        remote(
            part.at[j, p, other], from_core.at[j, p], part_send.at[j, p], part_recv.at[j, p], sibling
        ).wait_recv()
        for step in range(1, n_col):
            target = lax.rem(col + step, n_col)
            value = part[j, p, mpo, target] + from_core[j, p, target]
            to_col[j, p, step - 1] = value.astype(to_col.dtype)
            copy = remote(
                to_col.at[j, p, step - 1], from_col.at[j, p, col],
                col_send.at[j, p, step - 1], col_recv.at[j, p, col], {"col": target},
            )
            copy.start()
        image[p] = part[j, p, mpo, col] + from_core[j, p, col]

    def add_col(j, p):
        value = image[p]
        for step in range(1, n_col):
            source = lax.rem(col + step, n_col)
            remote(
                to_col.at[j, p, step - 1], from_col.at[j, p, source],
                col_send.at[j, p, step - 1], col_recv.at[j, p, source], {"col": source},
            ).wait_recv()
            value = value + from_col[j, p, source].astype(jnp.float32)
        value = value * live[p]
        image[p] = value
        return value

    def fold(value):
        return jnp.sum(value.reshape(rows // 8, 8, columns), axis=0)

    def gather(slots, own, peers, send, recv):
        block = slots.at[own]
        for step, (_, target) in enumerate(peers):
            copy = remote(block, block, send.at[step], recv.at[own], target)
            copy.start()
        for step, (index, target) in enumerate(peers):
            theirs = slots.at[index]
            remote(theirs, theirs, send.at[step], recv.at[index], target).wait_recv()

    def body(j, carry):
        exchange(j)
        norm = jnp.zeros((8, columns), jnp.float32)
        for p in range(sec_dev):
            norm = norm + fold(field[p] * field[p])

        @pl.when(j == 0)
        def _():
            load_right.wait()
            for p in range(sec_dev):
                for k in range(k_local):
                    block = right[k, p * width:(p + 1) * width, :]
                    right_t[p, k * stride:k * stride + columns, :] = block.T
            load_left.wait()

        relay(j)
        product(j, 0)
        for p in range(1, sec_dev):
            product(j, p)
            add_core(j, p - 1)
        add_core(j, sec_dev - 1)
        overlap = jnp.zeros((8, columns), jnp.float32)
        for p in range(sec_dev):
            overlap = overlap + fold(field[p] * add_col(j, p))
        team[j, mine] = jnp.concatenate(
            [jnp.sum(overlap, axis=0, keepdims=True), jnp.sum(norm, axis=0, keepdims=True)], axis=0
        )
        gather(team.at[j], mine, team_peers, team_send.at[j], team_recv.at[j])
        added = jnp.sum(team[j], axis=0)
        if not flat:
            line[j, row] = added
            gather(line.at[j], row, line_peers, line_send.at[j], line_recv.at[j])
            added = jnp.sum(line[j], axis=0)
        overlap = jnp.sum(added[0:1], keepdims=True)
        norm = jnp.sum(added[1:2], keepdims=True)
        beta = jnp.sqrt(norm + EPS)
        scale = 1.0 / beta
        alpha = overlap * scale * scale
        for p in range(sec_dev):
            v = field[p] * scale
            field[p] = image[p] * scale - alpha * v - beta * previous[p]
            previous[p] = v
        coef_ref[pl.ds(j, 1)] = jnp.broadcast_to(alpha, (1, LANES))
        coef_ref[pl.ds(STEPS - 1 + j, 1)] = jnp.where(
            j > 0, jnp.broadcast_to(beta, (1, LANES)), jnp.broadcast_to(alpha, (1, LANES))
        )

        return carry

    def drain(j, carry):
        for slot in range((n_row - 1) * cap):
            block = outgoing.at[j, slot]
            remote(block, block, row_send.at[j, slot], row_recv.at[j, 0], sibling).wait_send()
            remote(block, block, pass_send.at[j, slot], row_recv.at[j, 0], sibling).wait_send()
        remote(half.at[j], half.at[j], core_send.at[j], core_recv.at[j], sibling).wait_send()
        for p in range(sec_dev):
            block = part.at[j, p, other]
            remote(block, block, part_send.at[j, p], part_recv.at[j, p], sibling).wait_send()
            for step in range(1, n_col):
                block = to_col.at[j, p, step - 1]
                remote(
                    block, block, col_send.at[j, p, step - 1], col_recv.at[j, p, 0], sibling
                ).wait_send()
        block = team.at[j, mine]
        for step in range(len(team_peers)):
            remote(block, block, team_send.at[j, step], team_recv.at[j, 0], sibling).wait_send()
        if not flat:
            block = line.at[j, row]
            for step in range(len(line_peers)):
                remote(block, block, line_send.at[j, step], line_recv.at[j, 0], sibling).wait_send()
        return carry

    lax.fori_loop(0, STEPS, body, 0)

    copy = remote(field, final, final_send, final_recv, sibling)
    copy.start()
    for p in range(sec_dev):
        at = pl.multiple_of(p * width + mpo * rows, rows)
        resid_ref[pl.ds(at, rows)] = field[p]
    copy.wait_recv()
    for p in range(sec_dev):
        at = pl.multiple_of(p * width + other * rows, rows)
        resid_ref[pl.ds(at, rows)] = final[p]
    copy.wait_send()
    lax.fori_loop(0, STEPS, drain, 0)


def on_device(sizes, start, left_env, right_env, send_list, term_source, sector_len):
    n_row, n_col, n_mpo = sizes
    sec_dev = sector_len.shape[0]
    k_local, height, width = left_env.shape
    columns = start.shape[1]
    rows = width // n_mpo
    stride = max(columns, LANES)
    members = n_col * n_mpo
    team = n_row * members if n_row * members <= FLAT else members
    slots = send_list.shape[1]
    cap = slots // n_row
    away = max((n_row - 1) * cap, 1)
    bf, f32 = jnp.bfloat16, jnp.float32
    dma = pltpu.SemaphoreType.DMA
    hbm = pl.BlockSpec(memory_space=pl.ANY)
    smem = pl.BlockSpec(memory_space=pltpu.SMEM)
    vmem = pl.BlockSpec(memory_space=pltpu.VMEM)
    send = jnp.bfloat16
    resid, coef = pl.pallas_call(
        functools.partial(kernel, sizes),
        out_shape=(
            jax.ShapeDtypeStruct((height, columns), f32),
            jax.ShapeDtypeStruct((8, LANES), f32),
        ),
        in_specs=[hbm, hbm, hbm, smem, smem, smem],
        out_specs=(vmem, vmem),
        scratch_shapes=[
            pltpu.VMEM((k_local, height, width), bf),
            pltpu.VMEM((k_local, height, columns), bf),
            pltpu.VMEM((sec_dev, k_local * stride, width), bf),
            pltpu.VMEM((sec_dev, rows, columns), f32),
            pltpu.VMEM((sec_dev, rows, columns), f32),
            pltpu.VMEM((sec_dev, rows, columns), f32),
            pltpu.VMEM((STEPS, sec_dev, rows, columns), bf),
            pltpu.VMEM((STEPS, sec_dev + slots, width, columns), bf),
            pltpu.VMEM((STEPS, away, rows, columns), bf),
            pltpu.VMEM((sec_dev, width, k_local * stride), bf),
            pltpu.VMEM((STEPS, sec_dev, n_mpo, n_col, rows, columns), f32),
            pltpu.VMEM((STEPS, sec_dev, n_col, rows, columns), f32),
            pltpu.VMEM((STEPS, sec_dev, n_col, rows, columns), send),
            pltpu.VMEM((STEPS, sec_dev, n_col, rows, columns), send),
            pltpu.VMEM((STEPS, team, 2, columns), f32),
            pltpu.VMEM((STEPS, n_row, 2, columns), f32),
            pltpu.VMEM((sec_dev, rows, columns), f32),
            dma((sec_dev + 2,)),
            dma((STEPS,)),
            dma((STEPS,)),
            dma((STEPS, away)),
            dma((STEPS, slots)),
            dma((STEPS, away)),
            dma((STEPS, slots)),
            dma((STEPS, sec_dev)),
            dma((STEPS, sec_dev)),
            dma((STEPS, sec_dev, n_col)),
            dma((STEPS, sec_dev, n_col)),
            dma((STEPS, team)),
            dma((STEPS, team)),
            dma((STEPS, n_row)),
            dma((STEPS, n_row)),
            dma,
            dma,
        ],
        compiler_params=pltpu.CompilerParams(
            collective_id=0, has_side_effects=True, vmem_limit_bytes=56 * 1024 * 1024
        ),
    )(start, left_env, right_env, send_list, term_source, sector_len)
    return resid, coef[:2 * STEPS - 1, 0]


def solution(mesh):
    placed = (
        P(("groups", "row"), "col"),
        P("mpo", ("groups", "row"), None),
        P("mpo", ("groups", "row"), "col"),
        P(("groups", "row"), None),
        P(("groups", "row"), "mpo"),
        P(("groups", "row")),
    )
    sizes = (mesh.shape["row"], mesh.shape["col"], mesh.shape["mpo"])
    return jax.shard_map(
        functools.partial(on_device, sizes),
        mesh=mesh,
        in_specs=placed,
        out_specs=(P(("groups", "row"), "col"), P("groups")),
        check_vma=False,
    )
```

```python
import functools

import jax
import jax.numpy as jnp
from jax import lax
from jax.experimental import pallas as pl
from jax.experimental.pallas import tpu as pltpu
from jax.sharding import PartitionSpec as P

STEPS = 3
LANES = 128
EPS = 1e-06
FLAT = 16
MESH = pl.DeviceIdType.MESH


def kernel(
    sizes,
    start_ref,
    left_hbm,
    right_hbm,
    send_ref,
    term_ref,
    len_ref,
    resid_ref,
    coef_ref,
    left,
    right,
    right_t,
    field,
    previous,
    image,
    half,
    pool,
    outgoing,
    inner,
    part,
    from_core,
    to_col,
    from_col,
    across,
    team,
    line,
    final,
    load_sem,
    core_send,
    core_recv,
    row_send,
    row_recv,
    pass_send,
    pass_recv,
    part_send,
    part_recv,
    col_send,
    col_recv,
    across_send,
    across_recv,
    team_send,
    team_recv,
    line_send,
    line_recv,
    final_send,
    final_recv,
):
    n_row, n_col, n_mpo = sizes
    k_local, _, width = left_hbm.shape
    sec_dev, rows, columns = field.shape
    cap = send_ref.shape[1] // n_row
    stride = right_t.shape[1] // k_local
    members = n_col * n_mpo
    row = lax.axis_index("row")
    col = lax.axis_index("col")
    mpo = lax.axis_index("mpo")
    other = lax.rem(mpo + 1, 2)
    mine = col * n_mpo + mpo
    my_rows = pl.ds(pl.multiple_of(mpo * rows, rows), rows)
    sibling = {"mpo": other}

    flat = team.shape[1] == n_row * members
    team_peers = []
    for step in range(1, team.shape[1]):
        if flat:
            index = lax.rem(row * members + mine + step, n_row * members)
            target = {
                "row": index // members,
                "col": lax.rem(index // n_mpo, n_col),
                "mpo": lax.rem(index, n_mpo),
            }
        else:
            index = lax.rem(mine + step, members)
            target = {"col": index // n_mpo, "mpo": lax.rem(index, n_mpo)}
        team_peers.append((index, target))
    line_peers = []
    for step in range(1, n_row):
        index = lax.rem(row + step, n_row)
        line_peers.append((index, {"row": index}))
    if flat:
        mine = row * members + mine
    greeted = team_peers if flat else team_peers + line_peers

    def remote(src, dst, send, recv, target):
        return pltpu.make_async_remote_copy(
            src_ref=src, dst_ref=dst, send_sem=send, recv_sem=recv,
            device_id=target, device_id_type=MESH,
        )

    loads = []
    for p in range(sec_dev):
        at = pl.multiple_of(p * width + mpo * rows, rows)
        loads.append(pltpu.make_async_copy(start_ref.at[pl.ds(at, rows)], field.at[p], load_sem.at[p]))
    load_right = pltpu.make_async_copy(right_hbm, right, load_sem.at[sec_dev])
    load_left = pltpu.make_async_copy(left_hbm, left, load_sem.at[sec_dev + 1])
    for copy in loads:
        copy.start()
    load_right.start()
    load_left.start()

    barrier = pltpu.get_barrier_semaphore()

    for _, target in greeted:
        pl.semaphore_signal(barrier, inc=1, device_id=target, device_id_type=MESH)

    live = []
    for p in range(sec_dev):
        position = lax.broadcasted_iota(jnp.int32, (rows, columns), 0) + mpo * rows
        live.append((position < len_ref[p]).astype(jnp.float32))
    for copy in loads:
        copy.wait()
    for p in range(sec_dev):
        field[p] = field[p] * live[p]
    previous[...] = jnp.zeros_like(previous)
    for j in range(STEPS):
        for c in range(cap):
            pool[j, sec_dev + row * cap + c] = jnp.zeros((width, columns), jnp.bfloat16)
    if stride != columns:
        inner[...] = jnp.zeros_like(inner)
        right_t[...] = jnp.zeros_like(right_t)
    pl.semaphore_wait(barrier, len(greeted))

    def exchange(j):
        half[j] = field[...].astype(jnp.bfloat16)
        for step in range(1, n_row):
            target = lax.rem(row + step, n_row)
            for c in range(cap):
                slot = (step - 1) * cap + c
                pick = jnp.maximum(send_ref[0, target * cap + c], 0)
                outgoing[j, slot] = half[j, pick]
                place = sec_dev + row * cap + c
                copy = remote(
                    outgoing.at[j, slot], pool.at[j, place, my_rows],
                    row_send.at[j, slot], row_recv.at[j, row * cap + c], {"row": target},
                )
                copy.start()
        pool[j, pl.ds(0, sec_dev), my_rows] = half[j]
        own = remote(
            half.at[j], pool.at[j, pl.ds(0, sec_dev), my_rows], core_send.at[j], core_recv.at[j], sibling
        )
        own.start()
        for step in range(1, n_col):
            target = lax.rem(col + step, n_col)
            remote(
                field, across.at[j, col], across_send.at[j, step], across_recv.at[j, col],
                {"col": target},
            ).start()

    def relay(j):
        for step in range(1, n_row):
            source = lax.rem(row + step, n_row)
            for c in range(cap):
                slot = (step - 1) * cap + c
                place = sec_dev + source * cap + c
                block = pool.at[j, place, my_rows]
                remote(
                    outgoing.at[j, slot], block, row_send.at[j, slot],
                    row_recv.at[j, source * cap + c], {"row": source},
                ).wait_recv()
                copy = remote(
                    block, block, pass_send.at[j, slot], pass_recv.at[j, source * cap + c], sibling
                )
                copy.start()
        their_rows = pl.ds(pl.multiple_of(other * rows, rows), rows)
        remote(
            half.at[j], pool.at[j, pl.ds(0, sec_dev), their_rows], core_send.at[j], core_recv.at[j], sibling
        ).wait_recv()
        for step in range(1, n_row):
            source = lax.rem(row + step, n_row)
            for c in range(cap):
                slot = (step - 1) * cap + c
                block = pool.at[j, sec_dev + source * cap + c, their_rows]
                remote(
                    block, block, pass_send.at[j, slot], pass_recv.at[j, source * cap + c], sibling
                ).wait_recv()

    def product(j, p):
        for k in range(k_local):
            block = pool[j, term_ref[p, k]]
            value = jnp.dot(
                left[k, p * width:(p + 1) * width, :], block, preferred_element_type=jnp.float32
            )
            inner[p, :, k * stride:k * stride + columns] = value.astype(jnp.bfloat16)
        value = jnp.dot(inner[p], right_t[p], preferred_element_type=jnp.float32)
        for m in range(n_mpo):
            for c in range(n_col):
                part[j, p, m, c] = value[m * rows:(m + 1) * rows, c * columns:(c + 1) * columns]
        copy = remote(
            part.at[j, p, other], from_core.at[j, p], part_send.at[j, p], part_recv.at[j, p], sibling
        )
        copy.start()

    def add_core(j, p):
        remote(
            part.at[j, p, other], from_core.at[j, p], part_send.at[j, p], part_recv.at[j, p], sibling
        ).wait_recv()
        values = []
        for step in range(1, n_col):
            target = lax.rem(col + step, n_col)
            value = part[j, p, mpo, target] + from_core[j, p, target]
            values.append(value)
            to_col[j, p, step - 1] = value.astype(to_col.dtype)
            copy = remote(
                to_col.at[j, p, step - 1], from_col.at[j, p, col],
                col_send.at[j, p, step - 1], col_recv.at[j, p, col], {"col": target},
            )
            copy.start()
        value = part[j, p, mpo, col] + from_core[j, p, col]
        image[p] = value
        overlap = fold(field[p] * value)
        for step in range(1, n_col):
            source = lax.rem(col + step, n_col)
            if p == 0:
                theirs = across.at[j, source]
                remote(
                    theirs, theirs, across_send.at[j, step], across_recv.at[j, source], sibling
                ).wait_recv()
            overlap = overlap + fold(across[j, source, p] * values[step - 1])
        return overlap

    def add_col(j, p):
        value = image[p]
        for step in range(1, n_col):
            source = lax.rem(col + step, n_col)
            remote(
                to_col.at[j, p, step - 1], from_col.at[j, p, source],
                col_send.at[j, p, step - 1], col_recv.at[j, p, source], {"col": source},
            ).wait_recv()
            value = value + from_col[j, p, source].astype(jnp.float32)
        image[p] = value * live[p]

    def fold(value):
        return jnp.sum(value.reshape(rows // 8, 8, columns), axis=0)

    def spread(slots, own, peers, send, recv):
        block = slots.at[own]
        for step, (_, target) in enumerate(peers):
            remote(block, block, send.at[step], recv.at[own], target).start()

    def collect(slots, peers, send, recv):
        for step, (index, target) in enumerate(peers):
            theirs = slots.at[index]
            remote(theirs, theirs, send.at[step], recv.at[index], target).wait_recv()

    def body(j, carry):
        exchange(j)
        norm = jnp.zeros((8, columns), jnp.float32)
        for p in range(sec_dev):
            norm = norm + fold(field[p] * field[p])

        @pl.when(j == 0)
        def _():
            load_right.wait()
            for p in range(sec_dev):
                for k in range(k_local):
                    block = right[k, p * width:(p + 1) * width, :]
                    right_t[p, k * stride:k * stride + columns, :] = block.T
            load_left.wait()

        relay(j)
        product(j, 0)
        overlap = jnp.zeros((8, columns), jnp.float32)
        for p in range(1, sec_dev):
            product(j, p)
            overlap = overlap + add_core(j, p - 1)
        overlap = overlap + add_core(j, sec_dev - 1)
        team[j, mine] = jnp.concatenate(
            [jnp.sum(overlap, axis=0, keepdims=True), jnp.sum(norm, axis=0, keepdims=True)], axis=0
        )
        spread(team.at[j], mine, team_peers, team_send.at[j], team_recv.at[j])
        for p in range(sec_dev):
            add_col(j, p)
        collect(team.at[j], team_peers, team_send.at[j], team_recv.at[j])
        added = jnp.sum(team[j], axis=0)
        if not flat:
            line[j, row] = added
            spread(line.at[j], row, line_peers, line_send.at[j], line_recv.at[j])
            collect(line.at[j], line_peers, line_send.at[j], line_recv.at[j])
            added = jnp.sum(line[j], axis=0)
        overlap = jnp.sum(added[0:1], keepdims=True)
        norm = jnp.sum(added[1:2], keepdims=True)
        beta = jnp.sqrt(norm + EPS)
        scale = 1.0 / beta
        alpha = overlap * scale * scale
        for step in range(1, n_col):
            remote(
                field, across.at[j, col], across_send.at[j, step], across_recv.at[j, col], sibling
            ).wait_send()
        for p in range(sec_dev):
            v = field[p] * scale
            field[p] = image[p] * scale - alpha * v - beta * previous[p]
            previous[p] = v
        coef_ref[pl.ds(j, 1)] = jnp.broadcast_to(alpha, (1, LANES))
        coef_ref[pl.ds(STEPS - 1 + j, 1)] = jnp.where(
            j > 0, jnp.broadcast_to(beta, (1, LANES)), jnp.broadcast_to(alpha, (1, LANES))
        )

        return carry

    def drain(j, carry):
        for slot in range((n_row - 1) * cap):
            block = outgoing.at[j, slot]
            remote(block, block, row_send.at[j, slot], row_recv.at[j, 0], sibling).wait_send()
            remote(block, block, pass_send.at[j, slot], row_recv.at[j, 0], sibling).wait_send()
        remote(half.at[j], half.at[j], core_send.at[j], core_recv.at[j], sibling).wait_send()
        for p in range(sec_dev):
            block = part.at[j, p, other]
            remote(block, block, part_send.at[j, p], part_recv.at[j, p], sibling).wait_send()
            for step in range(1, n_col):
                block = to_col.at[j, p, step - 1]
                remote(
                    block, block, col_send.at[j, p, step - 1], col_recv.at[j, p, 0], sibling
                ).wait_send()
        block = team.at[j, mine]
        for step in range(len(team_peers)):
            remote(block, block, team_send.at[j, step], team_recv.at[j, 0], sibling).wait_send()
        if not flat:
            block = line.at[j, row]
            for step in range(len(line_peers)):
                remote(block, block, line_send.at[j, step], line_recv.at[j, 0], sibling).wait_send()
        return carry

    lax.fori_loop(0, STEPS, body, 0)

    copy = remote(field, final, final_send, final_recv, sibling)
    copy.start()
    for p in range(sec_dev):
        at = pl.multiple_of(p * width + mpo * rows, rows)
        resid_ref[pl.ds(at, rows)] = field[p]
    copy.wait_recv()
    for p in range(sec_dev):
        at = pl.multiple_of(p * width + other * rows, rows)
        resid_ref[pl.ds(at, rows)] = final[p]
    copy.wait_send()
    lax.fori_loop(0, STEPS, drain, 0)


def on_device(sizes, start, left_env, right_env, send_list, term_source, sector_len):
    n_row, n_col, n_mpo = sizes
    sec_dev = sector_len.shape[0]
    k_local, height, width = left_env.shape
    columns = start.shape[1]
    rows = width // n_mpo
    stride = max(columns, LANES)
    members = n_col * n_mpo
    team = n_row * members if n_row * members <= FLAT else members
    slots = send_list.shape[1]
    cap = slots // n_row
    away = max((n_row - 1) * cap, 1)
    bf, f32 = jnp.bfloat16, jnp.float32
    dma = pltpu.SemaphoreType.DMA
    hbm = pl.BlockSpec(memory_space=pl.ANY)
    smem = pl.BlockSpec(memory_space=pltpu.SMEM)
    vmem = pl.BlockSpec(memory_space=pltpu.VMEM)
    send = jnp.bfloat16
    resid, coef = pl.pallas_call(
        functools.partial(kernel, sizes),
        out_shape=(
            jax.ShapeDtypeStruct((height, columns), f32),
            jax.ShapeDtypeStruct((8, LANES), f32),
        ),
        in_specs=[hbm, hbm, hbm, smem, smem, smem],
        out_specs=(vmem, vmem),
        scratch_shapes=[
            pltpu.VMEM((k_local, height, width), bf),
            pltpu.VMEM((k_local, height, columns), bf),
            pltpu.VMEM((sec_dev, k_local * stride, width), bf),
            pltpu.VMEM((sec_dev, rows, columns), f32),
            pltpu.VMEM((sec_dev, rows, columns), f32),
            pltpu.VMEM((sec_dev, rows, columns), f32),
            pltpu.VMEM((STEPS, sec_dev, rows, columns), bf),
            pltpu.VMEM((STEPS, sec_dev + slots, width, columns), bf),
            pltpu.VMEM((STEPS, away, rows, columns), bf),
            pltpu.VMEM((sec_dev, width, k_local * stride), bf),
            pltpu.VMEM((STEPS, sec_dev, n_mpo, n_col, rows, columns), f32),
            pltpu.VMEM((STEPS, sec_dev, n_col, rows, columns), f32),
            pltpu.VMEM((STEPS, sec_dev, n_col, rows, columns), send),
            pltpu.VMEM((STEPS, sec_dev, n_col, rows, columns), send),
            pltpu.VMEM((STEPS, n_col, sec_dev, rows, columns), f32),
            pltpu.VMEM((STEPS, team, 2, columns), f32),
            pltpu.VMEM((STEPS, n_row, 2, columns), f32),
            pltpu.VMEM((sec_dev, rows, columns), f32),
            dma((sec_dev + 2,)),
            dma((STEPS,)),
            dma((STEPS,)),
            dma((STEPS, away)),
            dma((STEPS, slots)),
            dma((STEPS, away)),
            dma((STEPS, slots)),
            dma((STEPS, sec_dev)),
            dma((STEPS, sec_dev)),
            dma((STEPS, sec_dev, n_col)),
            dma((STEPS, sec_dev, n_col)),
            dma((STEPS, n_col)),
            dma((STEPS, n_col)),
            dma((STEPS, team)),
            dma((STEPS, team)),
            dma((STEPS, n_row)),
            dma((STEPS, n_row)),
            dma,
            dma,
        ],
        compiler_params=pltpu.CompilerParams(
            collective_id=0, has_side_effects=True, vmem_limit_bytes=56 * 1024 * 1024
        ),
    )(start, left_env, right_env, send_list, term_source, sector_len)
    return resid, coef[:2 * STEPS - 1, 0]


def solution(mesh):
    placed = (
        P(("groups", "row"), "col"),
        P("mpo", ("groups", "row"), None),
        P("mpo", ("groups", "row"), "col"),
        P(("groups", "row"), None),
        P(("groups", "row"), "mpo"),
        P(("groups", "row")),
    )
    sizes = (mesh.shape["row"], mesh.shape["col"], mesh.shape["mpo"])
    return jax.shard_map(
        functools.partial(on_device, sizes),
        mesh=mesh,
        in_specs=placed,
        out_specs=(P(("groups", "row"), "col"), P("groups")),
        check_vma=False,
    )
```

```python
import functools

import jax
import jax.numpy as jnp
from jax import lax
from jax.experimental import pallas as pl
from jax.experimental.pallas import tpu as pltpu
from jax.sharding import PartitionSpec as P

STEPS = 3
LANES = 128
EPS = 1e-06
FLAT = 16
MESH = pl.DeviceIdType.MESH


def kernel(
    sizes,
    start_ref,
    left_hbm,
    right_hbm,
    send_hbm,
    term_hbm,
    len_hbm,
    resid_ref,
    coef_ref,
    left,
    right,
    right_t,
    field,
    previous,
    image,
    half,
    pool,
    outgoing,
    inner,
    part,
    from_core,
    to_col,
    from_col,
    across,
    team,
    line,
    final,
    send_ref,
    term_ref,
    len_ref,
    load_sem,
    core_send,
    core_recv,
    row_send,
    row_recv,
    pass_send,
    pass_recv,
    part_send,
    part_recv,
    col_send,
    col_recv,
    across_send,
    across_recv,
    team_send,
    team_recv,
    line_send,
    line_recv,
    final_send,
    final_recv,
):
    n_row, n_col, n_mpo = sizes
    k_local, _, width = left_hbm.shape
    sec_dev, rows, columns = field.shape
    cap = send_ref.shape[1] // n_row
    stride = right_t.shape[1] // k_local
    members = n_col * n_mpo
    row = lax.axis_index("row")
    col = lax.axis_index("col")
    mpo = lax.axis_index("mpo")
    other = lax.rem(mpo + 1, 2)
    mine = col * n_mpo + mpo
    my_rows = pl.ds(pl.multiple_of(mpo * rows, rows), rows)
    sibling = {"mpo": other}

    flat = team.shape[1] == n_row * members
    turn = 1 - 2 * (row // max((n_row + 1) // 2, 1))
    team_peers = []
    for step in range(1, team.shape[1]):
        if flat:
            index = lax.rem(row * members + mine + n_row * members - turn * step, n_row * members)
            target = {
                "row": index // members,
                "col": lax.rem(index // n_mpo, n_col),
                "mpo": lax.rem(index, n_mpo),
            }
        else:
            index = lax.rem(mine + step, members)
            target = {"col": index // n_mpo, "mpo": lax.rem(index, n_mpo)}
        team_peers.append((index, target))
    line_peers = []
    for step in range(1, n_row):
        index = lax.rem(row + step, n_row)
        line_peers.append((index, {"row": index}))
    if flat:
        mine = row * members + mine
    greeted = team_peers if flat else team_peers + line_peers

    def remote(src, dst, send, recv, target):
        return pltpu.make_async_remote_copy(
            src_ref=src, dst_ref=dst, send_sem=send, recv_sem=recv,
            device_id=target, device_id_type=MESH,
        )

    loads = []
    for p in range(sec_dev):
        at = pl.multiple_of(p * width + mpo * rows, rows)
        loads.append(pltpu.make_async_copy(start_ref.at[pl.ds(at, rows)], field.at[p], load_sem.at[p]))
    load_right = pltpu.make_async_copy(right_hbm, right, load_sem.at[sec_dev])
    load_left = pltpu.make_async_copy(left_hbm, left, load_sem.at[sec_dev + 1])
    small = ((send_hbm, send_ref), (term_hbm, term_ref), (len_hbm, len_ref))
    for i, (src, dst) in enumerate(small):
        loads.append(pltpu.make_async_copy(src, dst, load_sem.at[sec_dev + 2 + i]))
    for copy in loads:
        copy.start()
    load_right.start()
    load_left.start()

    barrier = pltpu.get_barrier_semaphore()

    for _, target in greeted:
        pl.semaphore_signal(barrier, inc=1, device_id=target, device_id_type=MESH)

    for copy in loads:
        copy.wait()
    live = []
    for p in range(sec_dev):
        position = lax.broadcasted_iota(jnp.int32, (rows, columns), 0) + mpo * rows
        live.append((position < len_ref[p]).astype(jnp.float32))
    for p in range(sec_dev):
        field[p] = field[p] * live[p]
    previous[...] = jnp.zeros_like(previous)
    for j in range(STEPS):
        for c in range(cap):
            pool[j, sec_dev + row * cap + c] = jnp.zeros((width, columns), jnp.bfloat16)
    if stride != columns:
        inner[...] = jnp.zeros_like(inner)
        right_t[...] = jnp.zeros_like(right_t)
    pl.semaphore_wait(barrier, len(greeted))

    def exchange(j):
        half[j] = field[...].astype(jnp.bfloat16)
        for step in range(1, n_row):
            target = lax.rem(row - turn * step + n_row, n_row)
            for c in range(cap):
                slot = (step - 1) * cap + c
                pick = jnp.maximum(send_ref[0, target * cap + c], 0)
                outgoing[j, slot] = half[j, pick]
                place = sec_dev + row * cap + c
                copy = remote(
                    outgoing.at[j, slot], pool.at[j, place, my_rows],
                    row_send.at[j, slot], row_recv.at[j, row * cap + c], {"row": target},
                )
                copy.start()
        pool[j, pl.ds(0, sec_dev), my_rows] = half[j]
        own = remote(
            half.at[j], pool.at[j, pl.ds(0, sec_dev), my_rows], core_send.at[j], core_recv.at[j], sibling
        )
        own.start()
        for step in range(1, n_col):
            target = lax.rem(col + step, n_col)
            remote(
                field, across.at[j, col], across_send.at[j, step], across_recv.at[j, col],
                {"col": target},
            ).start()

    def relay(j):
        for step in range(1, n_row):
            source = lax.rem(row + turn * step + n_row, n_row)
            for c in range(cap):
                slot = (step - 1) * cap + c
                place = sec_dev + source * cap + c
                block = pool.at[j, place, my_rows]
                remote(
                    outgoing.at[j, slot], block, row_send.at[j, slot],
                    row_recv.at[j, source * cap + c], {"row": source},
                ).wait_recv()
                copy = remote(
                    block, block, pass_send.at[j, slot], pass_recv.at[j, source * cap + c], sibling
                )
                copy.start()
        their_rows = pl.ds(pl.multiple_of(other * rows, rows), rows)
        remote(
            half.at[j], pool.at[j, pl.ds(0, sec_dev), their_rows], core_send.at[j], core_recv.at[j], sibling
        ).wait_recv()
        for step in range(1, n_row):
            source = lax.rem(row + turn * step + n_row, n_row)
            for c in range(cap):
                slot = (step - 1) * cap + c
                block = pool.at[j, sec_dev + source * cap + c, their_rows]
                remote(
                    block, block, pass_send.at[j, slot], pass_recv.at[j, source * cap + c], sibling
                ).wait_recv()

    def product(j, p):
        for k in range(k_local):
            block = pool[j, term_ref[p, k]]
            value = jnp.dot(
                left[k, p * width:(p + 1) * width, :], block, preferred_element_type=jnp.float32
            )
            inner[p, :, k * stride:k * stride + columns] = value.astype(jnp.bfloat16)
        value = jnp.dot(inner[p], right_t[p], preferred_element_type=jnp.float32)
        for m in range(n_mpo):
            for c in range(n_col):
                part[j, p, m, c] = value[m * rows:(m + 1) * rows, c * columns:(c + 1) * columns]
        copy = remote(
            part.at[j, p, other], from_core.at[j, p], part_send.at[j, p], part_recv.at[j, p], sibling
        )
        copy.start()

    def add_core(j, p):
        remote(
            part.at[j, p, other], from_core.at[j, p], part_send.at[j, p], part_recv.at[j, p], sibling
        ).wait_recv()
        values = []
        for step in range(1, n_col):
            target = lax.rem(col + step, n_col)
            value = part[j, p, mpo, target] + from_core[j, p, target]
            values.append(value)
            to_col[j, p, step - 1] = value.astype(to_col.dtype)
            copy = remote(
                to_col.at[j, p, step - 1], from_col.at[j, p, col],
                col_send.at[j, p, step - 1], col_recv.at[j, p, col], {"col": target},
            )
            copy.start()
        value = part[j, p, mpo, col] + from_core[j, p, col]
        image[p] = value
        overlap = fold(field[p] * value)
        for step in range(1, n_col):
            source = lax.rem(col + step, n_col)
            if p == 0:
                theirs = across.at[j, source]
                remote(
                    theirs, theirs, across_send.at[j, step], across_recv.at[j, source], sibling
                ).wait_recv()
            overlap = overlap + fold(across[j, source, p] * values[step - 1])
        return overlap

    def add_col(j, p):
        value = image[p]
        for step in range(1, n_col):
            source = lax.rem(col + step, n_col)
            remote(
                to_col.at[j, p, step - 1], from_col.at[j, p, source],
                col_send.at[j, p, step - 1], col_recv.at[j, p, source], {"col": source},
            ).wait_recv()
            value = value + from_col[j, p, source].astype(jnp.float32)
        image[p] = value * live[p]

    def fold(value):
        return jnp.sum(value.reshape(rows // 8, 8, columns), axis=0)

    def spread(slots, own, peers, send, recv):
        block = slots.at[own]
        for step, (_, target) in enumerate(peers):
            remote(block, block, send.at[step], recv.at[own], target).start()

    def collect(slots, peers, send, recv):
        for step, (index, target) in enumerate(peers):
            theirs = slots.at[index]
            remote(theirs, theirs, send.at[step], recv.at[index], target).wait_recv()

    def drain(j):
        for slot in range((n_row - 1) * cap):
            block = outgoing.at[j, slot]
            remote(block, block, row_send.at[j, slot], row_recv.at[j, 0], sibling).wait_send()
            remote(block, block, pass_send.at[j, slot], row_recv.at[j, 0], sibling).wait_send()
        remote(half.at[j], half.at[j], core_send.at[j], core_recv.at[j], sibling).wait_send()
        for p in range(sec_dev):
            block = part.at[j, p, other]
            remote(block, block, part_send.at[j, p], part_recv.at[j, p], sibling).wait_send()
            for step in range(1, n_col):
                block = to_col.at[j, p, step - 1]
                remote(
                    block, block, col_send.at[j, p, step - 1], col_recv.at[j, p, 0], sibling
                ).wait_send()
        block = team.at[j, mine]
        for step in range(len(team_peers)):
            remote(block, block, team_send.at[j, step], team_recv.at[j, 0], sibling).wait_send()
        if not flat:
            block = line.at[j, row]
            for step in range(len(line_peers)):
                remote(block, block, line_send.at[j, step], line_recv.at[j, 0], sibling).wait_send()

    def body(j, carry):
        exchange(j)

        @pl.when(j > 0)
        def _():
            drain(j - 1)

        norm = jnp.zeros((8, columns), jnp.float32)
        for p in range(sec_dev):
            norm = norm + fold(field[p] * field[p])

        @pl.when(j == 0)
        def _():
            load_right.wait()
            for p in range(sec_dev):
                for k in range(k_local):
                    block = right[k, p * width:(p + 1) * width, :]
                    right_t[p, k * stride:k * stride + columns, :] = block.T
            load_left.wait()

        relay(j)
        product(j, 0)
        overlap = jnp.zeros((8, columns), jnp.float32)
        for p in range(1, sec_dev):
            product(j, p)
            overlap = overlap + add_core(j, p - 1)
        overlap = overlap + add_core(j, sec_dev - 1)
        team[j, mine] = jnp.concatenate(
            [jnp.sum(overlap, axis=0, keepdims=True), jnp.sum(norm, axis=0, keepdims=True)], axis=0
        )
        spread(team.at[j], mine, team_peers, team_send.at[j], team_recv.at[j])
        for p in range(sec_dev):
            add_col(j, p)
        collect(team.at[j], team_peers, team_send.at[j], team_recv.at[j])
        added = jnp.sum(team[j], axis=0)
        if not flat:
            line[j, row] = added
            spread(line.at[j], row, line_peers, line_send.at[j], line_recv.at[j])
            collect(line.at[j], line_peers, line_send.at[j], line_recv.at[j])
            added = jnp.sum(line[j], axis=0)
        overlap = jnp.sum(added[0:1], keepdims=True)
        norm = jnp.sum(added[1:2], keepdims=True)
        beta = jnp.sqrt(norm + EPS)
        scale = 1.0 / beta
        alpha = overlap * scale * scale
        for step in range(1, n_col):
            remote(
                field, across.at[j, col], across_send.at[j, step], across_recv.at[j, col], sibling
            ).wait_send()
        for p in range(sec_dev):
            v = field[p] * scale
            field[p] = image[p] * scale - alpha * v - beta * previous[p]
            previous[p] = v
        coef_ref[pl.ds(j, 1)] = jnp.broadcast_to(alpha, (1, LANES))
        coef_ref[pl.ds(STEPS - 1 + j, 1)] = jnp.where(
            j > 0, jnp.broadcast_to(beta, (1, LANES)), jnp.broadcast_to(alpha, (1, LANES))
        )

        return carry

    lax.fori_loop(0, STEPS, body, 0)

    copy = remote(field, final, final_send, final_recv, sibling)
    copy.start()
    for p in range(sec_dev):
        at = pl.multiple_of(p * width + mpo * rows, rows)
        resid_ref[pl.ds(at, rows)] = field[p]
    drain(STEPS - 1)
    copy.wait_recv()
    for p in range(sec_dev):
        at = pl.multiple_of(p * width + other * rows, rows)
        resid_ref[pl.ds(at, rows)] = final[p]
    copy.wait_send()


def on_device(sizes, start, left_env, right_env, send_list, term_source, sector_len):
    n_row, n_col, n_mpo = sizes
    sec_dev = sector_len.shape[0]
    k_local, height, width = left_env.shape
    columns = start.shape[1]
    rows = width // n_mpo
    stride = max(columns, LANES)
    members = n_col * n_mpo
    team = n_row * members if n_row * members <= FLAT else members
    slots = send_list.shape[1]
    cap = slots // n_row
    away = max((n_row - 1) * cap, 1)
    bf, f32 = jnp.bfloat16, jnp.float32
    dma = pltpu.SemaphoreType.DMA
    hbm = pl.BlockSpec(memory_space=pl.ANY)
    vmem = pl.BlockSpec(memory_space=pltpu.VMEM)
    send = jnp.bfloat16
    resid, coef = pl.pallas_call(
        functools.partial(kernel, sizes),
        out_shape=(
            jax.ShapeDtypeStruct((height, columns), f32),
            jax.ShapeDtypeStruct((8, LANES), f32),
        ),
        in_specs=[hbm] * 6,
        out_specs=(vmem, vmem),
        scratch_shapes=[
            pltpu.VMEM((k_local, height, width), bf),
            pltpu.VMEM((k_local, height, columns), bf),
            pltpu.VMEM((sec_dev, k_local * stride, width), bf),
            pltpu.VMEM((sec_dev, rows, columns), f32),
            pltpu.VMEM((sec_dev, rows, columns), f32),
            pltpu.VMEM((sec_dev, rows, columns), f32),
            pltpu.VMEM((STEPS, sec_dev, rows, columns), bf),
            pltpu.VMEM((STEPS, sec_dev + slots, width, columns), bf),
            pltpu.VMEM((STEPS, away, rows, columns), bf),
            pltpu.VMEM((sec_dev, width, k_local * stride), bf),
            pltpu.VMEM((STEPS, sec_dev, n_mpo, n_col, rows, columns), f32),
            pltpu.VMEM((STEPS, sec_dev, n_col, rows, columns), f32),
            pltpu.VMEM((STEPS, sec_dev, n_col, rows, columns), send),
            pltpu.VMEM((STEPS, sec_dev, n_col, rows, columns), send),
            pltpu.VMEM((STEPS, n_col, sec_dev, rows, columns), f32),
            pltpu.VMEM((STEPS, team, 2, columns), f32),
            pltpu.VMEM((STEPS, n_row, 2, columns), f32),
            pltpu.VMEM((sec_dev, rows, columns), f32),
            pltpu.SMEM(send_list.shape, jnp.int32),
            pltpu.SMEM(term_source.shape, jnp.int32),
            pltpu.SMEM(sector_len.shape, jnp.int32),
            dma((sec_dev + 5,)),
            dma((STEPS,)),
            dma((STEPS,)),
            dma((STEPS, away)),
            dma((STEPS, slots)),
            dma((STEPS, away)),
            dma((STEPS, slots)),
            dma((STEPS, sec_dev)),
            dma((STEPS, sec_dev)),
            dma((STEPS, sec_dev, n_col)),
            dma((STEPS, sec_dev, n_col)),
            dma((STEPS, n_col)),
            dma((STEPS, n_col)),
            dma((STEPS, team)),
            dma((STEPS, team)),
            dma((STEPS, n_row)),
            dma((STEPS, n_row)),
            dma,
            dma,
        ],
        compiler_params=pltpu.CompilerParams(
            collective_id=0, has_side_effects=True, vmem_limit_bytes=56 * 1024 * 1024
        ),
    )(start, left_env, right_env, send_list, term_source, sector_len)
    return resid, coef[:2 * STEPS - 1, 0]


def solution(mesh):
    placed = (
        P(("groups", "row"), "col"),
        P("mpo", ("groups", "row"), None),
        P("mpo", ("groups", "row"), "col"),
        P(("groups", "row"), None),
        P(("groups", "row"), "mpo"),
        P(("groups", "row")),
    )
    sizes = (mesh.shape["row"], mesh.shape["col"], mesh.shape["mpo"])
    return jax.shard_map(
        functools.partial(on_device, sizes),
        mesh=mesh,
        in_specs=placed,
        out_specs=(P(("groups", "row"), "col"), P("groups")),
        check_vma=False,
    )
```

```python
import functools

import jax
import jax.numpy as jnp
from jax import lax
from jax.experimental import pallas as pl
from jax.experimental.pallas import tpu as pltpu
from jax.sharding import PartitionSpec as P

STEPS = 3
LANES = 128
EPS = 1e-06
FLAT = 16
MESH = pl.DeviceIdType.MESH


def kernel(
    sizes,
    start_ref,
    left_hbm,
    right_hbm,
    send_hbm,
    term_hbm,
    len_hbm,
    resid_ref,
    coef_ref,
    left,
    right,
    right_t,
    field,
    previous,
    image,
    half,
    pool,
    outgoing,
    inner,
    part,
    from_core,
    to_col,
    from_col,
    across,
    team,
    line,
    final,
    send_ref,
    term_ref,
    len_ref,
    load_sem,
    core_send,
    core_recv,
    row_send,
    row_recv,
    pass_send,
    pass_recv,
    part_send,
    part_recv,
    col_send,
    col_recv,
    across_send,
    across_recv,
    team_send,
    team_recv,
    line_send,
    line_recv,
    final_send,
    final_recv,
):
    n_row, n_col, n_mpo = sizes
    k_local, _, width = left_hbm.shape
    sec_dev, rows, columns = field.shape
    cap = send_ref.shape[1] // n_row
    stride = right_t.shape[1] // k_local
    members = n_col * n_mpo
    row = lax.axis_index("row")
    col = lax.axis_index("col")
    mpo = lax.axis_index("mpo")
    other = lax.rem(mpo + 1, 2)
    mine = col * n_mpo + mpo
    my_rows = pl.ds(pl.multiple_of(mpo * rows, rows), rows)
    sibling = {"mpo": other}

    flat = team.shape[1] == n_row * members
    turn = 1 - 2 * (row // max((n_row + 1) // 2, 1))
    team_peers = []
    for step in range(1, team.shape[1]):
        if flat:
            index = lax.rem(row * members + mine + n_row * members - turn * step, n_row * members)
            target = {
                "row": index // members,
                "col": lax.rem(index // n_mpo, n_col),
                "mpo": lax.rem(index, n_mpo),
            }
        else:
            index = lax.rem(mine + step, members)
            target = {"col": index // n_mpo, "mpo": lax.rem(index, n_mpo)}
        team_peers.append((index, target))
    line_peers = []
    for step in range(1, n_row):
        index = lax.rem(row + step, n_row)
        line_peers.append((index, {"row": index}))
    if flat:
        mine = row * members + mine
    greeted = team_peers if flat else team_peers + line_peers

    def remote(src, dst, send, recv, target):
        return pltpu.make_async_remote_copy(
            src_ref=src, dst_ref=dst, send_sem=send, recv_sem=recv,
            device_id=target, device_id_type=MESH,
        )

    loads = []
    for p in range(sec_dev):
        at = pl.multiple_of(p * width + mpo * rows, rows)
        loads.append(pltpu.make_async_copy(start_ref.at[pl.ds(at, rows)], field.at[p], load_sem.at[p]))
    load_right = pltpu.make_async_copy(right_hbm, right, load_sem.at[sec_dev])
    load_left = pltpu.make_async_copy(left_hbm, left, load_sem.at[sec_dev + 1])
    small = ((send_hbm, send_ref), (term_hbm, term_ref), (len_hbm, len_ref))
    for i, (src, dst) in enumerate(small):
        loads.append(pltpu.make_async_copy(src, dst, load_sem.at[sec_dev + 2 + i]))
    for copy in loads:
        copy.start()
    load_right.start()
    load_left.start()

    barrier = pltpu.get_barrier_semaphore()

    for _, target in greeted:
        pl.semaphore_signal(barrier, inc=1, device_id=target, device_id_type=MESH)

    for copy in loads:
        copy.wait()
    live = []
    for p in range(sec_dev):
        position = lax.broadcasted_iota(jnp.int32, (rows, columns), 0) + mpo * rows
        live.append((position < len_ref[p]).astype(jnp.float32))
    for p in range(sec_dev):
        field[p] = field[p] * live[p]
    previous[...] = jnp.zeros_like(previous)
    for j in range(STEPS):
        for c in range(cap):
            pool[j, sec_dev + row * cap + c] = jnp.zeros((width, columns), jnp.bfloat16)
    if stride != columns:
        inner[...] = jnp.zeros_like(inner)
        right_t[...] = jnp.zeros_like(right_t)
    pl.semaphore_wait(barrier, len(greeted))

    def exchange(j):
        half[j] = field[...].astype(jnp.bfloat16)
        for step in range(1, n_row):
            target = lax.rem(row - turn * step + n_row, n_row)
            for c in range(cap):
                slot = (step - 1) * cap + c
                pick = jnp.maximum(send_ref[0, target * cap + c], 0)
                outgoing[j, slot] = half[j, pick]
                place = sec_dev + row * cap + c
                copy = remote(
                    outgoing.at[j, slot], pool.at[j, place, my_rows],
                    row_send.at[j, slot], row_recv.at[j, row * cap + c], {"row": target},
                )
                copy.start()
        pool[j, pl.ds(0, sec_dev), my_rows] = half[j]
        own = remote(
            half.at[j], pool.at[j, pl.ds(0, sec_dev), my_rows], core_send.at[j], core_recv.at[j], sibling
        )
        own.start()
        for step in range(1, n_col):
            target = lax.rem(col + step, n_col)
            remote(
                half.at[j], across.at[j, col], across_send.at[j, step], across_recv.at[j, col],
                {"col": target},
            ).start()

    def relay(j):
        for step in range(1, n_row):
            source = lax.rem(row + turn * step + n_row, n_row)
            for c in range(cap):
                slot = (step - 1) * cap + c
                place = sec_dev + source * cap + c
                block = pool.at[j, place, my_rows]
                remote(
                    outgoing.at[j, slot], block, row_send.at[j, slot],
                    row_recv.at[j, source * cap + c], {"row": source},
                ).wait_recv()
                copy = remote(
                    block, block, pass_send.at[j, slot], pass_recv.at[j, source * cap + c], sibling
                )
                copy.start()
        their_rows = pl.ds(pl.multiple_of(other * rows, rows), rows)
        remote(
            half.at[j], pool.at[j, pl.ds(0, sec_dev), their_rows], core_send.at[j], core_recv.at[j], sibling
        ).wait_recv()
        for step in range(1, n_row):
            source = lax.rem(row + turn * step + n_row, n_row)
            for c in range(cap):
                slot = (step - 1) * cap + c
                block = pool.at[j, sec_dev + source * cap + c, their_rows]
                remote(
                    block, block, pass_send.at[j, slot], pass_recv.at[j, source * cap + c], sibling
                ).wait_recv()

    def product(j, p):
        for k in range(k_local):
            block = pool[j, term_ref[p, k]]
            value = jnp.dot(
                left[k, p * width:(p + 1) * width, :], block, preferred_element_type=jnp.float32
            )
            inner[p, :, k * stride:k * stride + columns] = value.astype(jnp.bfloat16)
        value = jnp.dot(inner[p], right_t[p], preferred_element_type=jnp.float32)
        for m in range(n_mpo):
            for c in range(n_col):
                part[j, p, m, c] = value[m * rows:(m + 1) * rows, c * columns:(c + 1) * columns]
        copy = remote(
            part.at[j, p, other], from_core.at[j, p], part_send.at[j, p], part_recv.at[j, p], sibling
        )
        copy.start()

    def add_core(j, p):
        remote(
            part.at[j, p, other], from_core.at[j, p], part_send.at[j, p], part_recv.at[j, p], sibling
        ).wait_recv()
        values = []
        for step in range(1, n_col):
            target = lax.rem(col + step, n_col)
            value = part[j, p, mpo, target] + from_core[j, p, target]
            values.append(value)
            to_col[j, p, step - 1] = value.astype(to_col.dtype)
            copy = remote(
                to_col.at[j, p, step - 1], from_col.at[j, p, col],
                col_send.at[j, p, step - 1], col_recv.at[j, p, col], {"col": target},
            )
            copy.start()
        value = part[j, p, mpo, col] + from_core[j, p, col]
        image[p] = value
        overlap = fold(field[p] * value)
        for step in range(1, n_col):
            source = lax.rem(col + step, n_col)
            if p == 0:
                theirs = across.at[j, source]
                remote(
                    theirs, theirs, across_send.at[j, step], across_recv.at[j, source], sibling
                ).wait_recv()
            overlap = overlap + fold(across[j, source, p].astype(jnp.float32) * values[step - 1])
        return overlap

    def add_col(j, p):
        value = image[p]
        for step in range(1, n_col):
            source = lax.rem(col + step, n_col)
            remote(
                to_col.at[j, p, step - 1], from_col.at[j, p, source],
                col_send.at[j, p, step - 1], col_recv.at[j, p, source], {"col": source},
            ).wait_recv()
            value = value + from_col[j, p, source].astype(jnp.float32)
        image[p] = value * live[p]

    def fold(value):
        return jnp.sum(value.reshape(rows // 8, 8, columns), axis=0)

    def spread(slots, own, peers, send, recv):
        block = slots.at[own]
        for step, (_, target) in enumerate(peers):
            remote(block, block, send.at[step], recv.at[own], target).start()

    def collect(slots, peers, send, recv):
        for step, (index, target) in enumerate(peers):
            theirs = slots.at[index]
            remote(theirs, theirs, send.at[step], recv.at[index], target).wait_recv()

    def drain(j):
        for slot in range((n_row - 1) * cap):
            block = outgoing.at[j, slot]
            remote(block, block, row_send.at[j, slot], row_recv.at[j, 0], sibling).wait_send()
            remote(block, block, pass_send.at[j, slot], row_recv.at[j, 0], sibling).wait_send()
        remote(half.at[j], half.at[j], core_send.at[j], core_recv.at[j], sibling).wait_send()
        for p in range(sec_dev):
            block = part.at[j, p, other]
            remote(block, block, part_send.at[j, p], part_recv.at[j, p], sibling).wait_send()
            for step in range(1, n_col):
                block = to_col.at[j, p, step - 1]
                remote(
                    block, block, col_send.at[j, p, step - 1], col_recv.at[j, p, 0], sibling
                ).wait_send()
        block = team.at[j, mine]
        for step in range(len(team_peers)):
            remote(block, block, team_send.at[j, step], team_recv.at[j, 0], sibling).wait_send()
        if not flat:
            block = line.at[j, row]
            for step in range(len(line_peers)):
                remote(block, block, line_send.at[j, step], line_recv.at[j, 0], sibling).wait_send()

    def body(j, carry):
        exchange(j)

        @pl.when(j > 0)
        def _():
            drain(j - 1)

        norm = jnp.zeros((8, columns), jnp.float32)
        for p in range(sec_dev):
            norm = norm + fold(field[p] * field[p])

        @pl.when(j == 0)
        def _():
            load_right.wait()
            for p in range(sec_dev):
                for k in range(k_local):
                    block = right[k, p * width:(p + 1) * width, :]
                    right_t[p, k * stride:k * stride + columns, :] = block.T
            load_left.wait()

        relay(j)
        product(j, 0)
        overlap = jnp.zeros((8, columns), jnp.float32)
        for p in range(1, sec_dev):
            product(j, p)
            overlap = overlap + add_core(j, p - 1)
        overlap = overlap + add_core(j, sec_dev - 1)
        team[j, mine] = jnp.concatenate(
            [jnp.sum(overlap, axis=0, keepdims=True), jnp.sum(norm, axis=0, keepdims=True)], axis=0
        )
        spread(team.at[j], mine, team_peers, team_send.at[j], team_recv.at[j])
        for p in range(sec_dev):
            add_col(j, p)
        collect(team.at[j], team_peers, team_send.at[j], team_recv.at[j])
        added = jnp.sum(team[j], axis=0)
        if not flat:
            line[j, row] = added
            spread(line.at[j], row, line_peers, line_send.at[j], line_recv.at[j])
            collect(line.at[j], line_peers, line_send.at[j], line_recv.at[j])
            added = jnp.sum(line[j], axis=0)
        overlap = jnp.sum(added[0:1], keepdims=True)
        norm = jnp.sum(added[1:2], keepdims=True)
        beta = jnp.sqrt(norm + EPS)
        scale = 1.0 / beta
        alpha = overlap * scale * scale
        for step in range(1, n_col):
            remote(
                half.at[j], across.at[j, col], across_send.at[j, step], across_recv.at[j, col], sibling
            ).wait_send()
        for p in range(sec_dev):
            v = field[p] * scale
            field[p] = image[p] * scale - alpha * v - beta * previous[p]
            previous[p] = v
        coef_ref[pl.ds(j, 1)] = jnp.broadcast_to(alpha, (1, LANES))
        coef_ref[pl.ds(STEPS - 1 + j, 1)] = jnp.where(
            j > 0, jnp.broadcast_to(beta, (1, LANES)), jnp.broadcast_to(alpha, (1, LANES))
        )

        return carry

    lax.fori_loop(0, STEPS, body, 0)

    copy = remote(field, final, final_send, final_recv, sibling)
    copy.start()
    for p in range(sec_dev):
        at = pl.multiple_of(p * width + mpo * rows, rows)
        resid_ref[pl.ds(at, rows)] = field[p]
    drain(STEPS - 1)
    copy.wait_recv()
    for p in range(sec_dev):
        at = pl.multiple_of(p * width + other * rows, rows)
        resid_ref[pl.ds(at, rows)] = final[p]
    copy.wait_send()


def on_device(sizes, start, left_env, right_env, send_list, term_source, sector_len):
    n_row, n_col, n_mpo = sizes
    sec_dev = sector_len.shape[0]
    k_local, height, width = left_env.shape
    columns = start.shape[1]
    rows = width // n_mpo
    stride = max(columns, LANES)
    members = n_col * n_mpo
    team = n_row * members if n_row * members <= FLAT else members
    slots = send_list.shape[1]
    cap = slots // n_row
    away = max((n_row - 1) * cap, 1)
    bf, f32 = jnp.bfloat16, jnp.float32
    dma = pltpu.SemaphoreType.DMA
    hbm = pl.BlockSpec(memory_space=pl.ANY)
    vmem = pl.BlockSpec(memory_space=pltpu.VMEM)
    send = jnp.bfloat16
    resid, coef = pl.pallas_call(
        functools.partial(kernel, sizes),
        out_shape=(
            jax.ShapeDtypeStruct((height, columns), f32),
            jax.ShapeDtypeStruct((8, LANES), f32),
        ),
        in_specs=[hbm] * 6,
        out_specs=(vmem, vmem),
        scratch_shapes=[
            pltpu.VMEM((k_local, height, width), bf),
            pltpu.VMEM((k_local, height, columns), bf),
            pltpu.VMEM((sec_dev, k_local * stride, width), bf),
            pltpu.VMEM((sec_dev, rows, columns), f32),
            pltpu.VMEM((sec_dev, rows, columns), f32),
            pltpu.VMEM((sec_dev, rows, columns), f32),
            pltpu.VMEM((STEPS, sec_dev, rows, columns), bf),
            pltpu.VMEM((STEPS, sec_dev + slots, width, columns), bf),
            pltpu.VMEM((STEPS, away, rows, columns), bf),
            pltpu.VMEM((sec_dev, width, k_local * stride), bf),
            pltpu.VMEM((STEPS, sec_dev, n_mpo, n_col, rows, columns), f32),
            pltpu.VMEM((STEPS, sec_dev, n_col, rows, columns), f32),
            pltpu.VMEM((STEPS, sec_dev, n_col, rows, columns), send),
            pltpu.VMEM((STEPS, sec_dev, n_col, rows, columns), send),
            pltpu.VMEM((STEPS, n_col, sec_dev, rows, columns), bf),
            pltpu.VMEM((STEPS, team, 2, columns), f32),
            pltpu.VMEM((STEPS, n_row, 2, columns), f32),
            pltpu.VMEM((sec_dev, rows, columns), f32),
            pltpu.SMEM(send_list.shape, jnp.int32),
            pltpu.SMEM(term_source.shape, jnp.int32),
            pltpu.SMEM(sector_len.shape, jnp.int32),
            dma((sec_dev + 5,)),
            dma((STEPS,)),
            dma((STEPS,)),
            dma((STEPS, away)),
            dma((STEPS, slots)),
            dma((STEPS, away)),
            dma((STEPS, slots)),
            dma((STEPS, sec_dev)),
            dma((STEPS, sec_dev)),
            dma((STEPS, sec_dev, n_col)),
            dma((STEPS, sec_dev, n_col)),
            dma((STEPS, n_col)),
            dma((STEPS, n_col)),
            dma((STEPS, team)),
            dma((STEPS, team)),
            dma((STEPS, n_row)),
            dma((STEPS, n_row)),
            dma,
            dma,
        ],
        compiler_params=pltpu.CompilerParams(
            collective_id=0, has_side_effects=True, vmem_limit_bytes=56 * 1024 * 1024
        ),
    )(start, left_env, right_env, send_list, term_source, sector_len)
    return resid, coef[:2 * STEPS - 1, 0]


def solution(mesh):
    placed = (
        P(("groups", "row"), "col"),
        P("mpo", ("groups", "row"), None),
        P("mpo", ("groups", "row"), "col"),
        P(("groups", "row"), None),
        P(("groups", "row"), "mpo"),
        P(("groups", "row")),
    )
    sizes = (mesh.shape["row"], mesh.shape["col"], mesh.shape["mpo"])
    return jax.shard_map(
        functools.partial(on_device, sizes),
        mesh=mesh,
        in_specs=placed,
        out_specs=(P(("groups", "row"), "col"), P("groups")),
        check_vma=False,
    )
```
